32 devices in a mesh: chain: 8 (over z, core), grp: 4 (over y, x).
Axes of the slice: x: 2, y: 2, z: 4, core: 2. Of those that a mesh axis runs over, the one named last changes fastest.
Arguments:
- query_raw: bfloat16 [4096, 4096], P(('chain', 'grp')), may hold values from -6 to 6
- key_raw: bfloat16 [4096, 4096], P(('chain', 'grp')), may hold values from -6 to 6
- value_raw: bfloat16 [4096, 4096], P(('chain', 'grp')), may hold values from -6 to 6
- grad_out: bfloat16 [4096, 4096], P(('chain', 'grp')), may hold values from -6 to 6
- query_kernel: bfloat16 [4, 4096], replicated, may hold values from -3 to 3
- key_kernel: bfloat16 [4, 4096], replicated, may hold values from -3 to 3
- value_kernel: bfloat16 [4, 4096], replicated, may hold values from -3 to 3
Outputs:
- query_grad: bfloat16 [4096, 4096], P(('chain', 'grp'))
- key_grad: bfloat16 [4096, 4096], P(('chain', 'grp'))
- value_grad: bfloat16 [4096, 4096], P(('chain', 'grp'))
The draws below stay inside these ranges and needn't reach their ends.
All inputs are finite; a program needn't handle non-finite values.
Results may differ from the reference program's by a relative error of at most 0.011.
Values may be sent and summed in bfloat16 or wider, within the bound.
No kernel may reach another device: no remote copies, remote signals or barrier semaphores. Data moves between devices by JAX's collectives and lax.ppermute only.
A program may use at most 128 MiB of HBM per device.

```python
import jax
import jax.numpy as jnp
from jax import lax

H = 32
HEAD = 128
D = 4096
BLOCK = 1024
KERNEL = 4
TOKENS = 4096


def levels(stream_key, dims, cuts, low, high):
    factor_of, own = 1.0, jax.random.fold_in(stream_key, 6)
    for dim, blocks in cuts:
        steps = jnp.exp(jax.random.uniform(jax.random.fold_in(own, dim), (blocks,), jnp.float32, low / len(cuts), high / len(cuts)))
        factor_of = factor_of * jnp.repeat(steps, dims[dim] // blocks).reshape([-1 if axis == dim else 1 for axis in range(len(dims))])
    return factor_of


def scatter_about(rng, dims, spread, most, pieces=(), kind=jnp.bfloat16):
    array = jax.random.normal(rng, dims, jnp.float32) * spread
    if len(pieces) > 0:
        array = levels(rng, dims, pieces, -0.22, 0.18) * array
    return jnp.clip(array, min=-most, max=most).astype(kind)


def setup_inputs(seed: int = 0) -> dict:
    key_of = jax.random.split(jax.random.key(seed), 8)
    query_raw = scatter_about(key_of[0], (TOKENS, D), 1.0, 6.0, ((0, 32),))
    key_raw = scatter_about(key_of[1], (TOKENS, D), 1.0, 6.0, ((0, 32),))
    value_raw = scatter_about(key_of[2], (TOKENS, D), 1.0, 6.0, ((0, 32),))
    grad_out = scatter_about(key_of[3], (TOKENS, D), 1.0, 6.0, ((0, 32),))
    query_kernel = scatter_about(key_of[4], (KERNEL, D), 0.5, 3.0)
    key_kernel = scatter_about(key_of[5], (KERNEL, D), 0.5, 3.0)
    value_kernel = scatter_about(key_of[6], (KERNEL, D), 0.5, 3.0)
    return dict(query_raw=query_raw, key_raw=key_raw, value_raw=value_raw, grad_out=grad_out, query_kernel=query_kernel, key_kernel=key_kernel, value_kernel=value_kernel)


def shifted_down(field, offset):
    if offset == 0:
        return field
    filler = jnp.zeros((offset,) + field.shape[1:], field.dtype)
    return jnp.concatenate([filler, field[: field.shape[0] - offset]], 0)


def shifted_up(field, offset):
    if offset == 0:
        return field
    filler = jnp.zeros((offset,) + field.shape[1:], field.dtype)
    return jnp.concatenate([field[offset:], filler], 0)


def conv_forward(raw, kernel):
    inputs = raw.astype(jnp.float32)
    taps = kernel.astype(jnp.float32)
    total = taps[0][None, :] * inputs
    for offset in range(1, KERNEL):
        total = total + taps[offset][None, :] * shifted_down(inputs, offset)
    return total.astype(jnp.bfloat16)


def conv_backward(grads, kernel):
    taps = kernel.astype(jnp.float32)
    total = taps[0][None, :] * grads
    for offset in range(1, KERNEL):
        total = total + taps[offset][None, :] * shifted_up(grads, offset)
    return total.astype(jnp.bfloat16)


def head_grads(packed):
    highest = lax.Precision.HIGHEST
    queries, keys, values, cotangent = [piece.astype(jnp.float32) for piece in packed]
    span = min(BLOCK, TOKENS)
    blocks = TOKENS // span
    queries = queries.reshape(blocks, span, HEAD)
    keys = keys.reshape(blocks, span, HEAD)
    values = values.reshape(blocks, span, HEAD)
    cotangent = cotangent.reshape(blocks, span, HEAD)
    state_blocks = jnp.einsum("bsd,bse->bde", keys, values, precision=highest)
    grad_blocks = jnp.einsum("bsd,bse->bde", queries, cotangent, precision=highest)
    state_before = jnp.cumsum(state_blocks, 0) - state_blocks
    grad_after = jnp.sum(grad_blocks, 0)[None] - jnp.cumsum(grad_blocks, 0)
    state_before = state_before.astype(jnp.bfloat16).astype(jnp.float32)
    grad_after = grad_after.astype(jnp.bfloat16).astype(jnp.float32)
    lower = jnp.arange(span)[:, None] >= jnp.arange(span)[None, :]

    def one_block(items):
        query_block, key_block, value_block, cot_block, state_block, after_block = items
        scores = jnp.dot(cot_block, value_block.T, precision=highest)
        scores = jnp.where(lower, scores, 0.0).astype(jnp.bfloat16).astype(jnp.float32)
        similar = jnp.dot(query_block, key_block.T, precision=highest)
        similar = jnp.where(lower, similar, 0.0).astype(jnp.bfloat16).astype(jnp.float32)
        query_part = jnp.dot(scores, key_block, precision=highest) + jnp.dot(cot_block, state_block.T, precision=highest)
        key_part = jnp.dot(scores.T, query_block, precision=highest) + jnp.dot(value_block, after_block.T, precision=highest)
        value_part = jnp.dot(similar.T, cot_block, precision=highest) + jnp.dot(key_block, after_block, precision=highest)
        return jnp.stack([query_part, key_part, value_part])

    result = lax.map(one_block, (queries, keys, values, cotangent, state_before, grad_after))
    return result.transpose(1, 0, 2, 3).reshape(3, TOKENS, HEAD)


def reference(query_raw, key_raw, value_raw, grad_out, query_kernel, key_kernel, value_kernel):
    scale = float(HEAD * TOKENS) ** -0.5
    feature_query = conv_forward(query_raw, query_kernel)
    feature_key = conv_forward(key_raw, key_kernel)
    feature_value = conv_forward(value_raw, value_kernel)

    def by_heads(field):
        return field.reshape(TOKENS, H, HEAD).transpose(1, 0, 2)

    per_head = lax.map(head_grads, (by_heads(feature_query), by_heads(feature_key), by_heads(feature_value), by_heads(grad_out)))
    grads = per_head.transpose(1, 2, 0, 3).reshape(3, TOKENS, D) * scale
    return (conv_backward(grads[0], query_kernel), conv_backward(grads[1], key_kernel), conv_backward(grads[2], value_kernel))
```

```python
import functools
import math

import jax
import jax.numpy as jnp
from jax import lax
from jax.experimental import pallas as pl
from jax.experimental.pallas import tpu as pltpu
from jax.sharding import Mesh, PartitionSpec as P

HEAD = 128
KERNEL = 4
REACH = KERNEL - 1
CORES = 2
PAD = 8
EDGE = 16
CHUNKS = 4
STEP_HEADS = 4

F32 = jnp.float32
BF16 = jnp.bfloat16


def dot(a, b, ca, cb):
    return lax.dot_general(a, b, (((ca,), (cb,)), ((), ())), preferred_element_type=F32)


def states_kernel(
    q_ref, k_ref, v_ref, g_ref, prev_ref, next_ref, tq_ref, tk_ref, tv_ref,
    qf_ref, kf_ref, vf_ref, ge_ref, s_ref, x_ref,
):
    rows, width = q_ref.shape
    ext = rows + EDGE
    prev = prev_ref[...].astype(F32)
    after = next_ref[...].astype(F32)
    parts = ((q_ref, tq_ref, qf_ref), (k_ref, tk_ref, kf_ref), (v_ref, tv_ref, vf_ref))
    for i, (raw, tap_ref, out) in enumerate(parts):
        taps = tap_ref[...].astype(F32)
        x_ref[i, PAD - REACH : PAD] = prev[REACH * i : REACH * (i + 1)]
        x_ref[i, PAD : PAD + rows] = raw[...].astype(F32)
        x_ref[i, PAD + rows :] = jnp.zeros((EDGE, width), F32)
        x_ref[i, PAD + rows : PAD + rows + REACH] = after[REACH * i : REACH * (i + 1)]
        mixed = taps[0:1] * x_ref[i, PAD : PAD + ext]
        for j in range(1, KERNEL):
            mixed = mixed + taps[j : j + 1] * x_ref[i, PAD - j : PAD - j + ext]
        out[...] = mixed.astype(BF16)
    edge = jnp.concatenate([after[REACH * 3 : REACH * 4], jnp.zeros((EDGE - REACH, width), F32)], 0)
    ge_ref[...] = edge.astype(BF16)
    for h in range(width // HEAD):
        col = slice(h * HEAD, (h + 1) * HEAD)
        s_ref[h, 0] = dot(vf_ref[:rows, col], kf_ref[:rows, col], 0, 0).astype(BF16)
        s_ref[h, 1] = dot(g_ref[:, col], qf_ref[:rows, col], 0, 0).astype(BF16)


def grads_kernel(
    scale, alias, qf_ref, kf_ref, vf_ref, g_ref, ge_ref, s_ref, tq_ref, tk_ref, tv_ref, *rest
):
    dq_ref, dk_ref, dv_ref, d_ref = rest[3:] if alias else rest
    rows, width = g_ref.shape
    ext = rows + EDGE

    def order(shape):
        return lax.broadcasted_iota(jnp.int32, shape, 0), lax.broadcasted_iota(jnp.int32, shape, 1)

    row, col = order((ext, rows))
    lower = row >= col
    row, col = order((rows, rows))
    upper = col >= row
    row, col = order((EDGE, EDGE))
    edge_lower = row >= col
    edge_strict = col < row
    for h in range(width // HEAD):
        c = slice(h * HEAD, (h + 1) * HEAD)
        q, qe = qf_ref[:rows, c], qf_ref[rows:, c]
        k, ke = kf_ref[:rows, c], kf_ref[rows:, c]
        v, ve = vf_ref[:rows, c], vf_ref[rows:, c]
        g, ge = g_ref[:, c], ge_ref[:, c]
        vk, gq = s_ref[h, 0], s_ref[h, 1]
        gx = jnp.concatenate([g, ge], 0)
        scores = jnp.where(lower, dot(gx, v, 1, 1), 0.0).astype(BF16)
        d_ref[0, :, c] = dot(
            jnp.concatenate([scores, gx], 1), jnp.concatenate([k, vk], 0), 1, 0
        )
        scores_e = jnp.where(edge_lower, dot(ge, ve, 1, 1), 0.0).astype(BF16)
        d_ref[0, rows:, c] += dot(scores_e, ke, 1, 0)
        scores_t = jnp.where(upper, dot(v, g, 1, 1), 0.0).astype(BF16)
        d_ref[1, :rows, c] = dot(
            jnp.concatenate([scores_t, v], 1), jnp.concatenate([q, gq], 0), 1, 0
        )
        strict = jnp.where(edge_strict, dot(ve, ge, 1, 1), 0.0).astype(BF16)
        d_ref[1, rows:, c] = dot(ve, gq, 1, 0) - dot(strict, qe, 1, 0)
        similar_t = jnp.where(upper, dot(k, q, 1, 1), 0.0).astype(BF16)
        d_ref[2, :rows, c] = dot(similar_t, g, 1, 0) + dot(k, gq, 1, 1)
        strict = jnp.where(edge_strict, dot(ke, qe, 1, 1), 0.0).astype(BF16)
        d_ref[2, rows:, c] = dot(ke, gq, 1, 1) - dot(strict, ge, 1, 0)
    for i, (tap_ref, out) in enumerate(((tq_ref, dq_ref), (tk_ref, dk_ref), (tv_ref, dv_ref))):
        taps = tap_ref[...].astype(F32) * scale
        total = taps[0:1] * d_ref[i, 0:rows]
        for j in range(1, KERNEL):
            total = total + taps[j : j + 1] * d_ref[i, j : j + rows]
        out[...] = total.astype(BF16)


def states_call(chunk, heads, raws, prev, after, taps):
    rows = raws[0].shape[0]
    step = min(STEP_HEADS, heads)
    steps, width = heads // step, step * HEAD
    first = chunk * steps

    def wide(n):
        return pl.BlockSpec((n, width), lambda i: (0, first + i))

    def out(n):
        return pl.BlockSpec((n, width), lambda i: (0, i))

    ext = rows + EDGE
    return pl.pallas_call(
        states_kernel,
        grid=(steps,),
        in_specs=[wide(rows)] * 4 + [wide(EDGE)] * 2 + [wide(KERNEL)] * 3,
        out_specs=[out(ext)] * 3
        + [out(EDGE), pl.BlockSpec((step, 2, HEAD, HEAD), lambda i: (i, 0, 0, 0))],
        out_shape=[jax.ShapeDtypeStruct((ext, heads * HEAD), BF16)] * 3
        + [
            jax.ShapeDtypeStruct((EDGE, heads * HEAD), BF16),
            jax.ShapeDtypeStruct((heads, 2, HEAD, HEAD), BF16),
        ],
        scratch_shapes=[pltpu.VMEM((3, PAD + ext, width), F32)],
        compiler_params=pltpu.CompilerParams(vmem_limit_bytes=32 * 1024 * 1024),
        cost_estimate=pl.CostEstimate(
            flops=4 * heads * rows * HEAD * HEAD + 24 * heads * rows * HEAD,
            bytes_accessed=2 * heads * HEAD * (7 * rows + 2 * HEAD + 96),
            transcendentals=0,
        ),
        name="states",
    )(*raws, prev, after, *taps)


def grads_call(chunk, heads, total_width, scale, feats, g, state, taps, outs):
    rows = g.shape[0]
    step = min(STEP_HEADS, heads)
    steps, width = heads // step, step * HEAD
    first = chunk * steps
    ext = rows + EDGE

    def wide(n):
        return pl.BlockSpec((n, width), lambda i: (0, first + i))

    def own(n):
        return pl.BlockSpec((n, width), lambda i: (0, i))

    alias = outs is not None
    specs = [own(ext)] * 3 + [wide(rows), own(EDGE)]
    specs += [pl.BlockSpec((step, 2, HEAD, HEAD), lambda i: (i, 0, 0, 0))] + [wide(KERNEL)] * 3
    args = [*feats[:3], g, feats[3], state, *taps]
    aliases = {}
    if alias:
        aliases = {len(args) + i: i for i in range(3)}
        specs += [pl.BlockSpec(memory_space=pl.ANY)] * 3
        args += list(outs)
    return pl.pallas_call(
        functools.partial(grads_kernel, scale, alias),
        grid=(steps,),
        in_specs=specs,
        out_specs=[wide(rows)] * 3,
        out_shape=[jax.ShapeDtypeStruct((rows, total_width), BF16)] * 3,
        input_output_aliases=aliases,
        scratch_shapes=[pltpu.VMEM((3, ext, width), F32)],
        compiler_params=pltpu.CompilerParams(vmem_limit_bytes=32 * 1024 * 1024),
        cost_estimate=pl.CostEstimate(
            flops=20 * heads * rows * HEAD * HEAD,
            bytes_accessed=2 * heads * HEAD * (7 * rows + 2 * HEAD + 96),
            transcendentals=0,
        ),
        name="grads",
    )(*args)


def plane_sums(states):
    wide = states.astype(F32)
    return jnp.sum(wide[:, :, 0], 0), jnp.sum(wide[:, :, 1], 0)


def plane_scan(own_kv, own_gq):
    planes = lax.axis_size("z")
    place = lax.axis_index("z")
    kv, gq = own_kv, own_gq
    half = 1
    while half < planes:
        high = (place // half) % 2 == 1
        payload = jnp.where(high, gq, kv).astype(BF16)
        got = []
        for k in range(half):
            pairs = []
            for base in range(0, planes, 2 * half):
                pairs += [
                    (base + half - 1, base + half + k),
                    (base + half, base + half - 1 - k),
                ]
            got.append(lax.ppermute(payload, "z", pairs).astype(F32))
        arrived = sum(got[1:], got[0])
        kv = kv + jnp.where(high, arrived, 0.0)
        gq = gq + jnp.where(high, 0.0, arrived)
        half *= 2
    return kv - own_kv, gq - own_gq


def member_states(states, before, after):
    wide = states.astype(F32)
    members = wide.shape[0]
    kv, gq = [], []
    run = before
    for m in range(members):
        kv.append(run)
        run = run + wide[m, :, 0]
    run = after
    for m in reversed(range(members)):
        gq.append(run)
        run = run + wide[m, :, 1]
    gq.reverse()
    return jnp.stack([jnp.stack(kv), jnp.stack(gq)], 2).astype(BF16)


def local(query_raw, key_raw, value_raw, grad_out, query_kernel, key_kernel, value_kernel):
    rows, total_width = query_raw.shape
    z, grp = lax.axis_size("z"), lax.axis_size("grp")
    devices = z * CORES * grp
    members = CORES * grp
    scale = float(HEAD * rows * devices) ** (-0.5)
    heads_all = total_width // HEAD
    chunks = math.gcd(CHUNKS, heads_all // members)
    heads = heads_all // chunks
    everyone = ("z", "core", "grp")
    plane = ("core", "grp")
    raws = (query_raw, key_raw, value_raw, grad_out)
    taps = (query_kernel, key_kernel, value_kernel)

    up = [(i, i + 1) for i in range(devices - 1)]
    down = [(i + 1, i) for i in range(devices - 1)]
    tail = jnp.concatenate([r[rows - REACH :] for r in raws[:3]], 0)
    tail = jnp.pad(tail, ((0, EDGE - 3 * REACH), (0, 0)))
    lead = jnp.concatenate([r[:REACH] for r in raws], 0)
    lead = jnp.pad(lead, ((0, EDGE - 4 * REACH), (0, 0)))
    prev = lax.ppermute(tail, everyone, up)
    after = lax.ppermute(lead, everyone, down)

    feats, states = [], []
    for c in range(chunks):
        *f, s = states_call(c, heads, raws, prev, after, taps)
        feats.append(f)
        states.append(lax.all_to_all(s, plane, 0, 0, tiled=True))
    backs = []
    for c in range(chunks):
        s = states[c].reshape(members, heads // members, 2, HEAD, HEAD)
        own_kv, own_gq = plane_sums(s)
        before, later = plane_scan(own_kv, own_gq)
        back = member_states(s, before, later).reshape(heads, 2, HEAD, HEAD)
        backs.append(lax.all_to_all(back, plane, 0, 0, tiled=True))
    outs = None
    for c in range(chunks):
        outs = grads_call(c, heads, total_width, scale, feats[c], grad_out, backs[c], taps, outs)
    return tuple(outs)


def solution(mesh):
    chain, grp = mesh.shape["chain"], mesh.shape["grp"]
    split = Mesh(mesh.devices.reshape(chain // CORES, CORES, grp), ("z", "core", "grp"))
    tokens = P(("z", "core", "grp"), None)
    return jax.shard_map(
        local,
        mesh=split,
        in_specs=(tokens,) * 4 + (P(),) * 3,
        out_specs=(tokens,) * 3,
        check_vma=False,
    )
```

```python
import functools
import math

import jax
import jax.numpy as jnp
from jax import lax
from jax.experimental import pallas as pl
from jax.experimental.pallas import tpu as pltpu
from jax.sharding import Mesh, PartitionSpec as P

HEAD = 128
KERNEL = 4
REACH = KERNEL - 1
CORES = 2
PAD = 8
EDGE = 16
MIB = 1024 * 1024

F32 = jnp.float32
BF16 = jnp.bfloat16
MEMBER, PLANE = 0, 1


def dot(a, b, ca, cb):
    return lax.dot_general(a, b, (((ca,), (cb,)), ((), ())), preferred_element_type=F32)


def shape(dims, dtype=BF16):
    return jax.ShapeDtypeStruct(dims, dtype)


def params():
    return pltpu.CompilerParams(vmem_limit_bytes=60 * MIB)


def cost(flops, moved):
    return pl.CostEstimate(flops=int(flops), bytes_accessed=int(moved), transcendentals=0)


def pack_kernel(ql, kl, vl, qf, kf, vf, gf, tail_ref, lead_ref):
    def rows_of(refs, start, total):
        parts = [r[...].astype(F32)[start : start + REACH] for r in refs]
        fill = jnp.zeros((total - REACH * len(refs), parts[0].shape[1]), F32)
        return jnp.concatenate(parts + [fill], 0).astype(BF16)

    tail_ref[...] = rows_of((ql, kl, vl), EDGE - REACH, EDGE)
    lead_ref[...] = rows_of((qf, kf, vf, gf), 0, EDGE)


def pack(raws):
    rows, width = raws[0].shape
    last = pl.BlockSpec((EDGE, width), lambda i: (rows // EDGE - 1, 0))
    first = pl.BlockSpec((EDGE, width), lambda i: (0, 0))
    return pl.pallas_call(
        pack_kernel,
        grid=(1,),
        in_specs=[last] * 3 + [first] * 4,
        out_specs=[first] * 2,
        out_shape=[shape((EDGE, width))] * 2,
        compiler_params=params(),
        cost_estimate=cost(0, 9 * 2 * EDGE * width),
        name="pack",
    )(*raws[:3], *raws)


def states_kernel(peers, idx, cols, q_ref, k_ref, v_ref, g_ref, prev_ref, tq, tk, tv, *rest):
    outs, s_refs, x_ref = rest[:3], rest[3:-1], rest[-1]
    rows, width = q_ref.shape
    prev = prev_ref[...].astype(F32)
    states = []
    for h in range(width // HEAD):
        c = slice(h * HEAD, (h + 1) * HEAD)
        feats = []
        for i, (raw, tap_ref) in enumerate(((q_ref, tq), (k_ref, tk), (v_ref, tv))):
            taps = tap_ref[:, c].astype(F32)
            x_ref[h, i, PAD - REACH : PAD] = prev[REACH * i : REACH * (i + 1), c]
            x_ref[h, i, PAD:] = raw[:, c].astype(F32)
            mixed = taps[0:1] * x_ref[h, i, PAD:]
            for j in range(1, KERNEL):
                mixed = mixed + taps[j : j + 1] * x_ref[h, i, PAD - j : PAD - j + rows]
            feats.append(mixed.astype(BF16))
            outs[i][:, c] = feats[-1]
        qf, kf, vf = feats
        states.append((dot(vf, kf, 0, 0).astype(BF16), dot(g_ref[:, c], qf, 0, 0).astype(BF16)))
    for d in range(peers):

        @pl.when(pl.program_id(0) == d)
        def _():
            for h, (vk, gq) in enumerate(states):
                s_refs[d][h, 0] = vk
                s_refs[d][h, 1] = gq


def states_call(peers, heads, idx, cols, raws, prev, taps):
    rows = raws[0].shape[0]
    width = heads * HEAD

    def wide(n):
        return pl.BlockSpec((n, width), lambda i, x, p: (0, p[i]))

    def out(n):
        return pl.BlockSpec((n, width), lambda i, x, p: (0, i))

    whole = pl.BlockSpec((heads, 2, HEAD, HEAD), lambda i, x, p: (0, 0, 0, 0))
    return pl.pallas_call(
        functools.partial(states_kernel, peers),
        grid_spec=pltpu.PrefetchScalarGridSpec(
            num_scalar_prefetch=2,
            grid=(peers,),
            in_specs=[wide(rows)] * 4 + [wide(EDGE)] + [wide(KERNEL)] * 3,
            out_specs=[out(rows)] * 3 + [whole] * peers,
            scratch_shapes=[pltpu.VMEM((heads, 3, PAD + rows, HEAD), F32)],
        ),
        out_shape=[shape((rows, peers * width))] * 3 + [shape((heads, 2, HEAD, HEAD))] * peers,
        compiler_params=params(),
        cost_estimate=cost(
            4 * heads * peers * rows * HEAD * HEAD, 2 * heads * peers * HEAD * (7 * rows + 2 * HEAD)
        ),
        name="states",
    )(idx, cols, *raws, prev, *taps)


def intra_kernel(
    cols, qf, kf, vf, g_ref, ql, kl, vl, next_ref, tq, tk, tv, d_ref, ke_ref, ve_ref, ge_ref, x_ref
):
    rows, width = g_ref.shape
    after = next_ref[...].astype(F32)
    edges = []
    for i, (raw, tap_ref) in enumerate(((ql, tq), (kl, tk), (vl, tv))):
        taps = tap_ref[...].astype(F32)
        x_ref[i, :EDGE] = raw[...].astype(F32)
        x_ref[i, EDGE:] = jnp.zeros((EDGE, width), F32)
        x_ref[i, EDGE : EDGE + REACH] = after[REACH * i : REACH * (i + 1)]
        mixed = taps[0:1] * x_ref[i, EDGE:]
        for j in range(1, KERNEL):
            mixed = mixed + taps[j : j + 1] * x_ref[i, EDGE - j : 2 * EDGE - j]
        edges.append(mixed.astype(BF16))
    fill = jnp.zeros((EDGE - REACH, width), F32)
    edges.append(jnp.concatenate([after[3 * REACH : 4 * REACH], fill], 0).astype(BF16))
    qe_all, ke_all, ve_all, ge_all = edges
    ke_ref[...] = ke_all
    ve_ref[...] = ve_all
    ge_ref[...] = ge_all
    heads = width // HEAD

    def order(dims):
        return lax.broadcasted_iota(jnp.int32, dims, 0), lax.broadcasted_iota(jnp.int32, dims, 1)

    def stack(field):
        return jnp.concatenate([field[:, h * HEAD : (h + 1) * HEAD] for h in range(heads)], 0)

    qs, ks, vs, gs = [stack(field) for field in edges]
    row, col = order((heads * EDGE, heads * EDGE))
    same = row // EDGE == col // EDGE
    scores = dot(gs, vs, 1, 1)
    scores_t = dot(vs, gs, 1, 1)
    similar_t = dot(ks, qs, 1, 1)
    eq = dot(jnp.where(same & (row >= col), scores, 0.0).astype(BF16), ks, 1, 0)
    ek = dot(jnp.where(same & (col < row), scores_t, 0.0).astype(BF16), qs, 1, 0)
    ev = dot(jnp.where(same & (col < row), similar_t, 0.0).astype(BF16), gs, 1, 0)
    row, col = order((rows, rows))
    lower = row >= col
    upper = col >= row
    for h in range(heads):
        c = slice(h * HEAD, (h + 1) * HEAD)
        r = slice(h * EDGE, (h + 1) * EDGE)
        q, k, v, g = qf[:, c], kf[:, c], vf[:, c], g_ref[:, c]
        ge = ge_all[:, c]
        scores = jnp.where(lower, dot(g, v, 1, 1), 0.0).astype(BF16)
        d_ref[h, 0, :rows] = dot(scores, k, 1, 0)
        d_ref[h, 0, rows:] = dot(dot(ge, v, 1, 1).astype(BF16), k, 1, 0) + eq[r]
        scores_t = jnp.where(upper, dot(v, g, 1, 1), 0.0).astype(BF16)
        d_ref[h, 1, :rows] = dot(scores_t, q, 1, 0)
        d_ref[h, 1, rows:] = -ek[r]
        similar_t = jnp.where(upper, dot(k, q, 1, 1), 0.0).astype(BF16)
        d_ref[h, 2, :rows] = dot(similar_t, g, 1, 0)
        d_ref[h, 2, rows:] = -ev[r]


def intra_call(peers, heads, cols, feats, raws, after, taps):
    rows = raws[0].shape[0]
    width = heads * HEAD
    ext = rows + EDGE
    total = peers * width

    def wide(n, r=0):
        return pl.BlockSpec((n, width), lambda i, p: (r, p[i]))

    def own(n):
        return pl.BlockSpec((n, width), lambda i, p: (0, i))

    return pl.pallas_call(
        intra_kernel,
        grid_spec=pltpu.PrefetchScalarGridSpec(
            num_scalar_prefetch=1,
            grid=(peers,),
            in_specs=[own(rows)] * 3
            + [wide(rows)]
            + [wide(EDGE, rows // EDGE - 1)] * 3
            + [wide(EDGE)]
            + [wide(KERNEL)] * 3,
            out_specs=[pl.BlockSpec((heads, 3, ext, HEAD), lambda i, p: (i, 0, 0, 0))]
            + [own(EDGE)] * 3,
            scratch_shapes=[pltpu.VMEM((3, 2 * EDGE, width), F32)],
        ),
        out_shape=[shape((peers * heads, 3, ext, HEAD), F32)] + [shape((EDGE, total))] * 3,
        compiler_params=params(),
        cost_estimate=cost(
            12 * peers * heads * rows * HEAD * HEAD, peers * heads * HEAD * 4 * (3 * ext + 2 * rows)
        ),
        name="intra",
    )(cols, *feats, raws[3], *raws[:3], after, *taps)


def sums_kernel(members, idx, *refs):
    s_refs, outs = refs[:members], refs[members:]
    for h in range(outs[0].shape[0]):
        total = s_refs[0][h].astype(F32)
        for r in s_refs[1:]:
            total = total + r[h].astype(F32)
        for bit, out in enumerate(outs):
            low = (idx[PLANE] >> bit) & 1 == 0
            out[h] = jnp.where(low, total[0], total[1]).astype(BF16)


def members_kernel(members, planes, idx, *refs):
    s_refs, z_refs = refs[:members], refs[members : members + planes - 1]
    outs, run_ref = refs[members + planes - 1 : -1], refs[-1]
    for h in range(z_refs[0].shape[0]):
        kv = jnp.zeros((HEAD, HEAD), F32)
        gq = jnp.zeros((HEAD, HEAD), F32)
        for d in range(1, planes):
            got = z_refs[d - 1][h].astype(F32)
            earlier = (idx[PLANE] ^ d) < idx[PLANE]
            kv = kv + jnp.where(earlier, got, 0.0)
            gq = gq + jnp.where(earlier, 0.0, got)
        for d in range(members):
            run_ref[idx[MEMBER] ^ d] = s_refs[d][h].astype(F32)
        for m in range(members):
            own = run_ref[m, 0]
            run_ref[m, 0] = kv
            kv = kv + own
        for m in reversed(range(members)):
            own = run_ref[m, 1]
            run_ref[m, 1] = gq
            gq = gq + own
        for d in range(members):
            outs[d][h] = run_ref[idx[MEMBER] ^ d].astype(BF16)


def small_call(kernel, name, idx, args, outs, scratch=()):
    moved = sum(math.prod(x.shape) * x.dtype.itemsize for x in [*args, *outs])
    whole = pl.BlockSpec(memory_space=pltpu.VMEM)
    return pl.pallas_call(
        kernel,
        in_specs=[pl.BlockSpec(memory_space=pltpu.SMEM)] + [whole] * len(args),
        out_specs=[whole] * len(outs),
        out_shape=outs,
        scratch_shapes=scratch,
        compiler_params=pltpu.CompilerParams(vmem_limit_bytes=24 * MIB),
        cost_estimate=cost(0, moved),
        name=name,
    )(idx, *args)


def grads_kernel(
    scale, peers, alias, cols, kf, vf, g_ref, d_in, ke_ref, ve_ref, ge_ref, tq, tk, tv, *rest
):
    p_refs = rest[:peers]
    dq_ref, dk_ref, dv_ref, p_ref, d_ref = rest[peers + (3 if alias else 0) :]
    rows, width = g_ref.shape
    for d in range(peers):

        @pl.when(pl.program_id(0) == d)
        def _():
            p_ref[...] = p_refs[d][...]

    for h in range(width // HEAD):
        c = slice(h * HEAD, (h + 1) * HEAD)
        vk, gq = p_ref[h, 0], p_ref[h, 1]
        gx = jnp.concatenate([g_ref[:, c], ge_ref[:, c]], 0)
        vx = jnp.concatenate([vf[:, c], ve_ref[:, c]], 0)
        kx = jnp.concatenate([kf[:, c], ke_ref[:, c]], 0)
        d_ref[h, 0] = d_in[h, 0] + dot(gx, vk, 1, 0)
        d_ref[h, 1] = d_in[h, 1] + dot(vx, gq, 1, 0)
        d_ref[h, 2] = d_in[h, 2] + dot(kx, gq, 1, 1)
        for i, (tap_ref, out) in enumerate(((tq, dq_ref), (tk, dk_ref), (tv, dv_ref))):
            taps = tap_ref[:, c].astype(F32) * scale
            total = taps[0:1] * d_ref[h, i, 0:rows]
            for j in range(1, KERNEL):
                total = total + taps[j : j + 1] * d_ref[h, i, j : j + rows]
            out[:, c] = total.astype(BF16)


def grads_call(peers, heads, scale, cols, feats, g, intra, states, taps, outs):
    rows, total_width = g.shape
    width = heads * HEAD
    ext = rows + EDGE

    def wide(n):
        return pl.BlockSpec((n, width), lambda i, p: (0, p[i]))

    def own(n):
        return pl.BlockSpec((n, width), lambda i, p: (0, i))

    alias = outs is not None
    specs = [own(rows)] * 2 + [wide(rows)]
    specs += [pl.BlockSpec((heads, 3, ext, HEAD), lambda i, p: (i, 0, 0, 0))] + [own(EDGE)] * 3
    specs += [wide(KERNEL)] * 3
    specs += [pl.BlockSpec((heads, 2, HEAD, HEAD), lambda i, p: (0, 0, 0, 0))] * peers
    args = [feats[1], feats[2], g, *intra, *taps, *states]
    aliases = {}
    if alias:
        aliases = {1 + len(args) + i: i for i in range(3)}
        specs += [pl.BlockSpec(memory_space=pl.ANY)] * 3
        args += list(outs)
    return pl.pallas_call(
        functools.partial(grads_kernel, scale, peers, alias),
        grid_spec=pltpu.PrefetchScalarGridSpec(
            num_scalar_prefetch=1,
            grid=(peers,),
            in_specs=specs,
            out_specs=[wide(rows)] * 3,
            scratch_shapes=[
                pltpu.VMEM((heads, 2, HEAD, HEAD), BF16),
                pltpu.VMEM((heads, 3, ext, HEAD), F32),
            ],
        ),
        out_shape=[shape((rows, total_width))] * 3,
        input_output_aliases=aliases,
        compiler_params=params(),
        cost_estimate=cost(
            6 * heads * peers * ext * HEAD * HEAD, heads * peers * HEAD * (12 * ext + 12 * rows + 512)
        ),
        name="grads",
    )(cols, *args)


def local(query_raw, key_raw, value_raw, grad_out, query_kernel, key_kernel, value_kernel):
    rows, total_width = query_raw.shape
    planes, grp = lax.axis_size("z"), lax.axis_size("grp")
    members = CORES * grp
    devices = planes * members
    scale = float(HEAD * rows * devices) ** (-0.5)
    heads = total_width // HEAD // members
    everyone = ("z", "core", "grp")
    plane = ("core", "grp")
    raws = (query_raw, key_raw, value_raw, grad_out)
    taps = (query_kernel, key_kernel, value_kernel)
    me = lax.axis_index("core") * grp + lax.axis_index("grp")
    idx = jnp.stack([me, lax.axis_index("z")]).astype(jnp.int32)
    groups = [list(range(1, members, 2)), [*range(2, members, 2), 0]]
    cols = [(me ^ jnp.array(ds, jnp.int32)).astype(jnp.int32) for ds in groups]

    def swap(x, axes, count, d):
        return lax.ppermute(x, axes, [(i, i ^ d) for i in range(count)])

    def held(first, second):
        return lax.optimization_barrier((first, second))

    tail, lead = pack(raws)
    prev = lax.ppermute(tail, everyone, [(i, i + 1) for i in range(devices - 1)])
    after = lax.ppermute(lead, everyone, [(i + 1, i) for i in range(devices - 1)])

    feats, states = [], {}
    for n, ds in enumerate(groups):
        out = states_call(len(ds), heads, idx, cols[n], raws, prev, taps)
        feats.append(out[:3])
        for d, s in zip(ds, out[3:]):
            states[d] = swap(s, plane, members, d) if d else s
    intra = [None] * len(groups)
    intra[0] = intra_call(len(groups[0]), heads, cols[0], feats[0], raws, after, taps)
    states, intra[0] = held(states, intra[0])
    states = [states[d] for d in range(members)]
    bits = (planes - 1).bit_length()
    levels = small_call(
        functools.partial(sums_kernel, members),
        "sums",
        idx,
        states,
        [shape((heads, HEAD, HEAD))] * bits,
    )
    feats[1], levels = held(feats[1], levels)
    across = [swap(levels[d.bit_length() - 1], "z", planes, d) for d in range(1, planes)]
    intra[1] = intra_call(len(groups[1]), heads, cols[1], feats[1], raws, after, taps)
    across, intra[1] = held(across, intra[1])
    sent = small_call(
        functools.partial(members_kernel, members, planes),
        "members",
        idx,
        [*states, *across],
        [shape((heads, 2, HEAD, HEAD))] * members,
        [pltpu.VMEM((members, 2, HEAD, HEAD), F32)],
    )
    backs = {0: sent[0]}
    for d in [*groups[0], *groups[1]]:
        if d:
            backs[d] = swap(sent[d], plane, members, d)
    outs = None
    for n in (1, 0):
        ds = groups[n]
        outs = grads_call(
            len(ds), heads, scale, cols[n], feats[n], grad_out, intra[n], [backs[d] for d in ds], taps, outs
        )
    return tuple(outs)


def solution(mesh):
    chain, grp = mesh.shape["chain"], mesh.shape["grp"]
    split = Mesh(mesh.devices.reshape(chain // CORES, CORES, grp), ("z", "core", "grp"))
    tokens = P(("z", "core", "grp"), None)
    return jax.shard_map(
        local,
        mesh=split,
        in_specs=(tokens,) * 4 + (P(),) * 3,
        out_specs=(tokens,) * 3,
        check_vma=False,
    )
```

```python
import functools
import math

import jax
import jax.numpy as jnp
from jax import lax
from jax.experimental import pallas as pl
from jax.experimental.pallas import tpu as pltpu
from jax.sharding import Mesh, PartitionSpec as P

HEAD = 128
KERNEL = 4
REACH = KERNEL - 1
CORES = 2
PAD = 8
TILE = 16
EDGE = 16
MIB = 1024 * 1024

F32 = jnp.float32
BF16 = jnp.bfloat16


def dot(a, b, ca, cb):
    return lax.dot_general(a, b, (((ca,), (cb,)), ((), ())), preferred_element_type=F32)


def shape(dims, dtype=BF16):
    return jax.ShapeDtypeStruct(dims, dtype)


def far(x):
    return pltpu.with_memory_space_constraint(x, pltpu.HBM)


def params(mib=20):
    return pltpu.CompilerParams(vmem_limit_bytes=mib * MIB)


def cost(flops, moved):
    return pl.CostEstimate(flops=int(flops), bytes_accessed=int(moved), transcendentals=0)


def pack_kernel(q_ref, k_ref, v_ref, g_ref, tail_ref, lead_ref, x_ref, sems):
    rows = q_ref.shape[0]
    copies = []
    for i, ref in enumerate((q_ref, k_ref, v_ref)):
        copies.append((ref.at[pl.ds(rows - EDGE, EDGE)], x_ref.at[i]))
    for i, ref in enumerate((q_ref, k_ref, v_ref, g_ref)):
        copies.append((ref.at[pl.ds(0, EDGE)], x_ref.at[3 + i]))
    copies = [pltpu.make_async_copy(a, b, sems.at[i]) for i, (a, b) in enumerate(copies)]
    for copy in copies:
        copy.start()

    def rows_of(first, count, start):
        parts = [x_ref[first + i].astype(F32)[start : start + REACH] for i in range(count)]
        fill = jnp.zeros((EDGE - REACH * count, parts[0].shape[1]), F32)
        return jnp.concatenate(parts + [fill], 0).astype(BF16)

    for copy in copies[:3]:
        copy.wait()
    tail_ref[...] = rows_of(0, 3, EDGE - REACH)
    for copy in copies[3:]:
        copy.wait()
    lead_ref[...] = rows_of(3, 4, 0)


def pack(raws):
    width = raws[0].shape[1]
    return pl.pallas_call(
        pack_kernel,
        in_specs=[pl.BlockSpec(memory_space=pltpu.HBM)] * 4,
        out_specs=[pl.BlockSpec(memory_space=pltpu.VMEM)] * 2,
        out_shape=[shape((EDGE, width))] * 2,
        scratch_shapes=[pltpu.VMEM((7, EDGE, width), BF16), pltpu.SemaphoreType.DMA((7,))],
        compiler_params=params(),
        cost_estimate=cost(0, 9 * 2 * EDGE * width),
        name="pack",
    )(*[far(x) for x in raws])


def lanes(start, width=HEAD):
    return pl.ds(pl.multiple_of(start, HEAD), width)


class Copies:
    def __init__(self, sems):
        self.sems, self.count = sems, 0

    def start(self, source, target):
        copy = pltpu.make_async_copy(source, target, self.sems.at[self.count])
        self.count += 1
        copy.start()
        return copy


def wait(copies):
    for copy in copies:
        copy.wait()


HBM = pl.BlockSpec(memory_space=pltpu.HBM)
VMEM = pl.BlockSpec(memory_space=pltpu.VMEM)
SMEM = pl.BlockSpec(memory_space=pltpu.SMEM)


def marked_call(kernel, name, cols, near, remote, outs, scratch=(), flops=0, behind=(), aliases=()):
    args = [*near, *remote]
    hidden = len(behind)
    total = len(args) + len(outs)

    def body(cols, *refs):
        refs[hidden + total][0] = 0
        kernel(cols, *refs[hidden : hidden + total], *refs[hidden + total + 1 :])

    def out_spec(x):
        return HBM if getattr(x, "memory_space", None) == pltpu.HBM else VMEM

    moved = sum(math.prod(x.shape) * jnp.dtype(x.dtype).itemsize for x in [*args, *outs])
    *results, mark = pl.pallas_call(
        body,
        in_specs=[SMEM] * (1 + hidden) + [VMEM] * len(near) + [HBM] * len(remote),
        out_specs=[out_spec(x) for x in outs] + [SMEM],
        out_shape=[*outs, shape((1,), jnp.int32)],
        scratch_shapes=scratch,
        input_output_aliases={1 + hidden + i: o for i, o in aliases},
        compiler_params=params(),
        cost_estimate=cost(flops, moved),
        name=name,
    )(cols, *behind, *near, *[far(x) for x in remote])
    return results, mark


def conv(x, taps, raw, before, rows):
    x[PAD - REACH : PAD] = before
    x[PAD : PAD + raw.shape[0]] = raw.astype(F32)
    mixed = taps[0:1] * x[PAD : PAD + rows]
    for j in range(1, KERNEL):
        mixed = mixed + taps[j : j + 1] * x[PAD - j : PAD - j + rows]
    return mixed.astype(BF16)


def states_kernel(peers, heads, cols, prev_ref, tq, tk, tv, *rest):
    raws, s_refs = rest[:4], rest[4:-3]
    raw_ref, x_ref, sems = rest[-3:]
    rows, width = raw_ref.shape[2:]
    copies = Copies(sems)
    loads = []
    for p in range(peers):
        c = lanes(cols[p] * width, width)
        loads.append([copies.start(raw.at[:, c], raw_ref.at[p, i]) for i, raw in enumerate(raws)])
    for p in range(peers):
        wait(loads[p])
        for h in range(heads):
            c = lanes((cols[p] * heads + h) * HEAD)
            own = slice(h * HEAD, (h + 1) * HEAD)
            prev = prev_ref[:, c].astype(F32)
            qf, kf, vf = [
                conv(
                    x_ref.at[(p * heads + h) % 4, i],
                    tap_ref[:, c].astype(F32),
                    raw_ref[p, i, :, own],
                    prev[REACH * i : REACH * (i + 1)],
                    rows,
                )
                for i, tap_ref in enumerate((tq, tk, tv))
            ]
            s_refs[p][h, 0] = dot(vf, kf, 0, 0).astype(BF16)
            s_refs[p][h, 1] = dot(raw_ref[p, 3, :, own], qf, 0, 0).astype(BF16)


def states_call(peers, heads, cols, raws, prev, taps, behind):
    rows = raws[0].shape[0]
    return marked_call(
        functools.partial(states_kernel, peers, heads),
        "states",
        cols,
        [prev, *taps],
        raws,
        [shape((heads, 2, HEAD, HEAD))] * peers,
        [
            pltpu.VMEM((peers, 4, rows, heads * HEAD), BF16),
            pltpu.VMEM((4, 3, PAD + rows, HEAD), F32),
            pltpu.SemaphoreType.DMA((peers * 4,)),
        ],
        4 * peers * heads * rows * HEAD * HEAD,
        behind,
    )


def intra_kernel(
    peers, heads, cols, prev_ref, next_ref, tq, tk, tv, q_hbm, k_hbm, v_hbm, g_hbm, _,
    d_hbm, e_hbm, f_hbm, raw_ref, d_ref, e_ref, f_ref, x_ref, sems,
):
    rows, width = raw_ref.shape[2:]
    ext = rows + EDGE
    copies = Copies(sems)
    loads = []
    for p in range(peers):
        c = lanes(cols[p] * width, width)
        raws = (q_hbm, k_hbm, v_hbm, g_hbm)
        loads.append([copies.start(raw.at[:, c], raw_ref.at[p, i]) for i, raw in enumerate(raws)])

    def order(dims):
        return lax.broadcasted_iota(jnp.int32, dims, 0), lax.broadcasted_iota(jnp.int32, dims, 1)

    row, col = order((heads * EDGE, heads * EDGE))
    same = row // EDGE == col // EDGE
    edge_lower = same & (row >= col)
    edge_strict = same & (col < row)
    row, col = order((ext, rows))
    lower = row >= col
    row, col = order((rows, rows))
    upper = col >= row
    fill = jnp.zeros((EDGE - REACH, HEAD), F32)
    saves = []
    for p in range(peers):
        wait(loads[p])
        whole = []
        for h in range(heads):
            c = lanes((cols[p] * heads + h) * HEAD)
            own = slice(h * HEAD, (h + 1) * HEAD)
            prev = prev_ref[:, c].astype(F32)
            after = next_ref[:, c].astype(F32)
            feats = []
            for i, tap_ref in enumerate((tq, tk, tv)):
                x = x_ref.at[h, i]
                ahead = slice(REACH * i, REACH * (i + 1))
                x[PAD + rows : PAD + rows + REACH] = after[ahead]
                x[PAD + rows + REACH :] = fill
                taps = tap_ref[:, c].astype(F32)
                feats.append(conv(x, taps, raw_ref[p, i, :, own], prev[ahead], ext))
            edge = jnp.concatenate([after[3 * REACH : 4 * REACH], fill], 0).astype(BF16)
            feats.append(jnp.concatenate([raw_ref[p, 3, :, own], edge], 0))
            for i in range(3):
                e_ref[p, i, :, own] = feats[1 + i][rows:]
            for i in range(2):
                f_ref[p, i, :, own] = feats[1 + i][:rows]
            whole.append(feats)
        qs, ks, vs, gs = [jnp.concatenate([f[i][rows:] for f in whole], 0) for i in range(4)]
        scores = dot(gs, vs, 1, 1)
        scores_t = dot(vs, gs, 1, 1)
        similar_t = dot(ks, qs, 1, 1)
        eq = dot(jnp.where(edge_lower, scores, 0.0).astype(BF16), ks, 1, 0)
        ek = dot(jnp.where(edge_strict, scores_t, 0.0).astype(BF16), qs, 1, 0)
        ev = dot(jnp.where(edge_strict, similar_t, 0.0).astype(BF16), gs, 1, 0)
        for h in range(heads):
            r = slice(h * EDGE, (h + 1) * EDGE)
            q, k, v, gx = whole[h]
            q, k, v, g = q[:rows], k[:rows], v[:rows], gx[:rows]
            scores = dot(gx, v, 1, 1)
            part = dot(jnp.where(lower, scores, 0.0).astype(BF16), k, 1, 0)
            d_ref[p, h, 0, :rows] = part[:rows].astype(BF16)
            d_ref[p, h, 0, rows:] = (part[rows:] + eq[r]).astype(BF16)
            scores_t = jnp.where(upper, scores[:rows].T, 0.0).astype(BF16)
            d_ref[p, h, 1, :rows] = dot(scores_t, q, 1, 0).astype(BF16)
            d_ref[p, h, 1, rows:] = (-ek[r]).astype(BF16)
            similar_t = jnp.where(upper, dot(k, q, 1, 1), 0.0).astype(BF16)
            d_ref[p, h, 2, :rows] = dot(similar_t, g, 1, 0).astype(BF16)
            d_ref[p, h, 2, rows:] = (-ev[r]).astype(BF16)
        saves.append(copies.start(d_ref.at[p], d_hbm.at[p]))
        saves.append(copies.start(e_ref.at[p], e_hbm.at[p]))
        saves.append(copies.start(f_ref.at[p], f_hbm.at[p]))
    wait(saves)


def intra_call(peers, heads, cols, raws, prev, after, taps, arrived, behind):
    rows = raws[0].shape[0]
    ext = rows + EDGE
    width = heads * HEAD
    outs = [(peers, heads, 3, ext, HEAD), (peers, 3, EDGE, width), (peers, 2, rows, width)]
    return marked_call(
        functools.partial(intra_kernel, peers, heads),
        "intra",
        cols,
        [prev, after, *taps],
        [*raws, arrived],
        [pltpu.HBM(dims, BF16) for dims in outs],
        [pltpu.VMEM((peers, 4, rows, width), BF16)]
        + [pltpu.VMEM(dims, BF16) for dims in outs]
        + [
            pltpu.VMEM((heads, 3, PAD + ext, HEAD), F32),
            pltpu.SemaphoreType.DMA((peers * 7,)),
        ],
        12 * peers * heads * rows * HEAD * HEAD,
        behind,
    )


def sums_kernel(count, idx, *refs):
    s_refs, outs = refs[:count], refs[count:]
    heads = outs[0].shape[0]
    for h in range(heads):
        total = 0.0
        for r in s_refs:
            total = total + r[h].astype(F32)
        for bit, out in enumerate(outs):
            low = (idx[0] >> bit) & 1 == 0
            out[h] = jnp.where(low, total[0], total[1]).astype(BF16)


def members_kernel(count, planes, places, idx, *refs):
    s_refs, z_refs = refs[:count], refs[count : count + planes - 1]
    outs = refs[count + planes - 1 :]

    def share(condition):
        return jnp.where(condition, 1.0, 0.0)

    lower = [share((idx[0] ^ d) < idx[0]) for d in range(1, planes)]
    weights = [
        [
            (share(idx[1 + e] < idx[1 + place]), share(idx[1 + e] > idx[1 + place]))
            for e in range(count)
        ]
        for place in places
    ]
    for h in range(z_refs[0].shape[0]):
        for top in range(0, HEAD, TILE):
            r = slice(top, top + TILE)
            base = [0.0, 0.0]
            for z_ref, low in zip(z_refs, lower):
                got = z_ref[h, r].astype(F32)
                base = [base[0] + got * low, base[1] + got * (1.0 - low)]
            states = [[s_ref[h, i, r].astype(F32) for i in range(2)] for s_ref in s_refs]
            for out, shares in zip(outs, weights):
                for i in range(2):
                    total = base[i]
                    for state, weight in zip(states, shares):
                        total = total + state[i] * weight[i]
                    out[h, i, r] = total.astype(BF16)


def grads_kernel(scale, peers, heads, alias, cols, *refs):
    tq, tk, tv, d_ref, e_ref, f_ref, g_ref = refs[:7]
    p_refs = refs[7 : 7 + peers]
    outs, (out_ref, x_ref, sems) = refs[-6:-3], refs[-3:]
    rows, width = out_ref.shape[2:]
    copies = Copies(sems)
    saves = []
    for p in range(peers):
        for h in range(heads):
            c = lanes((cols[p] * heads + h) * HEAD)
            own = slice(h * HEAD, (h + 1) * HEAD)
            vk, gq = p_refs[p][h, 0], p_refs[p][h, 1]
            kx, vx, gx = [
                jnp.concatenate([field, e_ref[p, i, :, own]], 0)
                for i, field in enumerate((f_ref[p, 0, :, own], f_ref[p, 1, :, own], g_ref[:, c]))
            ]
            d = x_ref.at[h]
            d[0] = d_ref[p, h, 0].astype(F32) + dot(gx, vk, 1, 0)
            d[1] = d_ref[p, h, 1].astype(F32) + dot(vx, gq, 1, 0)
            d[2] = d_ref[p, h, 2].astype(F32) + dot(kx, gq, 1, 1)
            for i, tap_ref in enumerate((tq, tk, tv)):
                taps = tap_ref[:, c].astype(F32) * scale
                total = taps[0:1] * d[i, 0:rows]
                for j in range(1, KERNEL):
                    total = total + taps[j : j + 1] * d[i, j : j + rows]
                out_ref[p, i, :, own] = total.astype(BF16)
        c = lanes(cols[p] * width, width)
        saves += [copies.start(out_ref.at[p, i], outs[i].at[:, c]) for i in range(3)]
    wait(saves)


def grads_call(peers, heads, scale, cols, g, intra, states, taps, outs):
    rows, total_width = g.shape
    ext = rows + EDGE
    near = [*taps, *intra, g, *states]
    remote = []
    aliases = []
    if outs is not None:
        aliases = [(len(near) + i, i) for i in range(3)]
        remote = outs
    results, _ = marked_call(
        functools.partial(grads_kernel, scale, peers, heads, outs is not None),
        "grads",
        cols,
        near,
        remote,
        [pltpu.HBM((rows, total_width), BF16)] * 3,
        [
            pltpu.VMEM((peers, 3, rows, heads * HEAD), BF16),
            pltpu.VMEM((heads, 3, ext, HEAD), F32),
            pltpu.SemaphoreType.DMA((peers * 3,)),
        ],
        6 * heads * peers * ext * HEAD * HEAD,
        aliases=aliases,
    )
    return results


def local(query_raw, key_raw, value_raw, grad_out, query_kernel, key_kernel, value_kernel):
    rows, total_width = query_raw.shape
    planes = lax.axis_size("z")
    members = CORES * lax.axis_size("y") * lax.axis_size("x")
    devices = planes * members
    scale = float(HEAD * rows * devices) ** (-0.5)
    heads = total_width // HEAD // members
    everyone = ("z", "core", "y", "x")
    plane = ("core", "y", "x")
    raws = (query_raw, key_raw, value_raw, grad_out)
    taps = (query_kernel, key_kernel, value_kernel)
    x, z = lax.axis_index("x"), lax.axis_index("z")
    me = (lax.axis_index("core") * lax.axis_size("y") + lax.axis_index("y")) * lax.axis_size("x") + x
    width_y = lax.axis_size("y")
    steps = {d: (d % 2 > 0) + (d // 2 % width_y > 0) for d in range(members)}
    direct, diagonal, near = [[d for d in steps if steps[d] == n] for n in (1, 2, 0)]
    direct.sort(key=lambda d: (d // (2 * width_y), d))
    near.reverse()
    order = [*direct, *diagonal, *near]

    def numbers(ds):
        return (me ^ jnp.array(ds, jnp.int32)).astype(jnp.int32)

    idx = jnp.concatenate([z[None].astype(jnp.int32), numbers(order)])

    def swap(field, axes, count, d):
        return lax.ppermute(field, axes, [(i, i ^ d) for i in range(count)]) if d else field

    tail, lead = pack(raws)
    prev = lax.ppermute(tail, everyone, [(i, i + 1) for i in range(devices - 1)])
    after = lax.ppermute(lead, everyone, [(i + 1, i) for i in range(devices - 1)])

    states, mark = {}, []

    def make_states(ds, mark):
        out, mark = states_call(len(ds), heads, numbers(ds), raws, prev, taps, mark)
        states.update({d: swap(s, plane, members, d) for s, d in zip(out, ds)})
        return [mark]

    intra = {}

    def make_intra(ds, arrived, mark):
        args = (numbers(ds), raws, prev, after, taps, arrived, mark)
        intra[ds[0]], mark = intra_call(len(ds), heads, *args)
        return [mark]

    others = [*near, *diagonal]
    mark = make_states(direct, mark)
    mark = make_states(diagonal, mark)
    mark = make_states(near, mark)
    mark = make_intra(direct, states[direct[0]], mark)
    states = [states[d] for d in order]
    bits = (planes - 1).bit_length()
    levels, mark = marked_call(
        functools.partial(sums_kernel, members),
        "sums",
        idx,
        states,
        [],
        [shape((heads, HEAD, HEAD))] * bits,
        behind=mark,
    )
    across = [swap(levels[d.bit_length() - 1], "z", planes, d) for d in range(1, planes)]
    mark = make_intra(others, states[0], [mark])
    backs = {}
    for ds in (direct, [*diagonal, *near]):
        sent, mark = marked_call(
            functools.partial(members_kernel, members, planes, [order.index(d) for d in ds]),
            "members",
            idx,
            [*states, *across],
            [],
            [shape((heads, 2, HEAD, HEAD))] * len(ds),
            behind=mark,
        )
        mark = [mark]
        backs |= {d: swap(s, plane, members, d) for s, d in zip(sent, ds)}
    outs = None
    for ds in (direct, others):
        got = [backs[d] for d in ds]
        outs = grads_call(len(ds), heads, scale, numbers(ds), grad_out, intra[ds[0]], got, taps, outs)
    return tuple(outs)


def solution(mesh):
    chain, grp = mesh.shape["chain"], mesh.shape["grp"]
    sizes = (chain // CORES, CORES, grp // 2, 2)
    split = Mesh(mesh.devices.reshape(sizes), ("z", "core", "y", "x"))
    tokens = P(("z", "core", "y", "x"), None)
    return jax.shard_map(
        local,
        mesh=split,
        in_specs=(tokens,) * 4 + (P(),) * 3,
        out_specs=(tokens,) * 3,
        check_vma=False,
    )
```

```python
import functools
import math

import jax
import jax.numpy as jnp
from jax import lax
from jax.experimental import pallas as pl
from jax.experimental.pallas import tpu as pltpu
from jax.sharding import Mesh, PartitionSpec as P

HEAD = 128
KERNEL = 4
REACH = KERNEL - 1
CORES = 2
PAD = 8
TILE = 16
EDGE = 16
MIB = 1024 * 1024

F32 = jnp.float32
BF16 = jnp.bfloat16


def dot(a, b, ca, cb):
    return lax.dot_general(a, b, (((ca,), (cb,)), ((), ())), preferred_element_type=F32)


def shape(dims, dtype=BF16):
    return jax.ShapeDtypeStruct(dims, dtype)


def far(x):
    return pltpu.with_memory_space_constraint(x, pltpu.HBM)


def params(mib=20):
    return pltpu.CompilerParams(vmem_limit_bytes=mib * MIB)


def cost(flops, moved):
    return pl.CostEstimate(flops=int(flops), bytes_accessed=int(moved), transcendentals=0)


def pack_kernel(q_ref, k_ref, v_ref, g_ref, tail_ref, lead_ref, x_ref, sems):
    rows = q_ref.shape[0]
    copies = []
    for i, ref in enumerate((q_ref, k_ref, v_ref)):
        copies.append((ref.at[pl.ds(rows - EDGE, EDGE)], x_ref.at[i]))
    for i, ref in enumerate((q_ref, k_ref, v_ref, g_ref)):
        copies.append((ref.at[pl.ds(0, EDGE)], x_ref.at[3 + i]))
    copies = [pltpu.make_async_copy(a, b, sems.at[i]) for i, (a, b) in enumerate(copies)]
    for copy in copies:
        copy.start()

    def rows_of(first, count, start):
        parts = [x_ref[first + i].astype(F32)[start : start + REACH] for i in range(count)]
        fill = jnp.zeros((EDGE - REACH * count, parts[0].shape[1]), F32)
        return jnp.concatenate(parts + [fill], 0).astype(BF16)

    for copy in copies[:3]:
        copy.wait()
    tail_ref[...] = rows_of(0, 3, EDGE - REACH)
    for copy in copies[3:]:
        copy.wait()
    lead_ref[...] = rows_of(3, 4, 0)


def pack(raws):
    width = raws[0].shape[1]
    return pl.pallas_call(
        pack_kernel,
        in_specs=[pl.BlockSpec(memory_space=pltpu.HBM)] * 4,
        out_specs=[pl.BlockSpec(memory_space=pltpu.VMEM)] * 2,
        out_shape=[shape((EDGE, width))] * 2,
        scratch_shapes=[pltpu.VMEM((7, EDGE, width), BF16), pltpu.SemaphoreType.DMA((7,))],
        compiler_params=params(),
        cost_estimate=cost(0, 9 * 2 * EDGE * width),
        name="pack",
    )(*[far(x) for x in raws])


def lanes(start, width=HEAD):
    return pl.ds(pl.multiple_of(start, HEAD), width)


class Copies:
    def __init__(self, sems):
        self.sems, self.count = sems, 0

    def start(self, source, target):
        copy = pltpu.make_async_copy(source, target, self.sems.at[self.count])
        self.count += 1
        copy.start()
        return copy


def wait(copies):
    for copy in copies:
        copy.wait()


HBM = pl.BlockSpec(memory_space=pltpu.HBM)
VMEM = pl.BlockSpec(memory_space=pltpu.VMEM)
SMEM = pl.BlockSpec(memory_space=pltpu.SMEM)


def marked_call(
    kernel, name, cols, near, remote, outs, scratch=(), flops=0, behind=(), arrived=(), aliases=()
):
    args = [*near, *remote]
    hidden = len(behind) + len(arrived)
    total = len(args) + len(outs)

    def body(cols, *refs):
        refs[hidden + total][0] = 0
        kernel(cols, *refs[hidden : hidden + total], *refs[hidden + total + 1 :])

    def out_spec(x):
        return HBM if getattr(x, "memory_space", None) == pltpu.HBM else VMEM

    moved = sum(math.prod(x.shape) * jnp.dtype(x.dtype).itemsize for x in [*args, *outs])
    *results, mark = pl.pallas_call(
        body,
        in_specs=[SMEM] * (1 + len(behind))
        + [pl.BlockSpec(memory_space=pl.ANY)] * len(arrived)
        + [VMEM] * len(near)
        + [HBM] * len(remote),
        out_specs=[out_spec(x) for x in outs] + [SMEM],
        out_shape=[*outs, shape((1,), jnp.int32)],
        scratch_shapes=scratch,
        input_output_aliases={1 + hidden + i: o for i, o in aliases},
        compiler_params=params(),
        cost_estimate=cost(flops, moved),
        name=name,
    )(cols, *behind, *arrived, *near, *[far(x) for x in remote])
    return results, mark


def conv(x, taps, raw, before, rows):
    x[PAD - REACH : PAD] = before
    x[PAD : PAD + raw.shape[0]] = raw.astype(F32)
    mixed = taps[0:1] * x[PAD : PAD + rows]
    for j in range(1, KERNEL):
        mixed = mixed + taps[j : j + 1] * x[PAD - j : PAD - j + rows]
    return mixed.astype(BF16)


def states_kernel(peers, heads, cols, prev_ref, tq, tk, tv, *rest):
    raws, s_refs = rest[:4], rest[4:-3]
    raw_ref, x_ref, sems = rest[-3:]
    rows, width = raw_ref.shape[2:]
    copies = Copies(sems)
    loads = []
    for p in range(peers):
        c = lanes(cols[p] * width, width)
        loads.append([copies.start(raw.at[:, c], raw_ref.at[p, i]) for i, raw in enumerate(raws)])
    for p in range(peers):
        wait(loads[p])
        for h in range(heads):
            c = lanes((cols[p] * heads + h) * HEAD)
            own = slice(h * HEAD, (h + 1) * HEAD)
            prev = prev_ref[:, c].astype(F32)
            qf, kf, vf = [
                conv(
                    x_ref.at[(p * heads + h) % 4, i],
                    tap_ref[:, c].astype(F32),
                    raw_ref[p, i, :, own],
                    prev[REACH * i : REACH * (i + 1)],
                    rows,
                )
                for i, tap_ref in enumerate((tq, tk, tv))
            ]
            s_refs[p][h, 0] = dot(vf, kf, 0, 0).astype(BF16)
            s_refs[p][h, 1] = dot(raw_ref[p, 3, :, own], qf, 0, 0).astype(BF16)


def states_call(peers, heads, cols, raws, prev, taps, behind, arrived):
    rows = raws[0].shape[0]
    return marked_call(
        functools.partial(states_kernel, peers, heads),
        "states",
        cols,
        [prev, *taps],
        raws,
        [shape((heads, 2, HEAD, HEAD))] * peers,
        [
            pltpu.VMEM((peers, 4, rows, heads * HEAD), BF16),
            pltpu.VMEM((4, 3, PAD + rows, HEAD), F32),
            pltpu.SemaphoreType.DMA((peers * 4,)),
        ],
        4 * peers * heads * rows * HEAD * HEAD,
        behind,
        arrived,
    )


def intra_kernel(
    peers, heads, cols, prev_ref, next_ref, tq, tk, tv, q_hbm, k_hbm, v_hbm, g_hbm,
    d_hbm, e_hbm, f_hbm, raw_ref, d_ref, e_ref, f_ref, x_ref, sems,
):
    rows, width = raw_ref.shape[2:]
    ext = rows + EDGE
    copies = Copies(sems)
    loads = []
    for p in range(peers):
        c = lanes(cols[p] * width, width)
        raws = (q_hbm, k_hbm, v_hbm, g_hbm)
        loads.append([copies.start(raw.at[:, c], raw_ref.at[p, i]) for i, raw in enumerate(raws)])

    def order(dims):
        return lax.broadcasted_iota(jnp.int32, dims, 0), lax.broadcasted_iota(jnp.int32, dims, 1)

    row, col = order((heads * EDGE, heads * EDGE))
    same = row // EDGE == col // EDGE
    edge_lower = same & (row >= col)
    edge_strict = same & (col < row)
    row, col = order((ext, rows))
    lower = row >= col
    row, col = order((rows, rows))
    upper = col >= row
    fill = jnp.zeros((EDGE - REACH, HEAD), F32)
    saves = []
    for p in range(peers):
        wait(loads[p])
        whole = []
        for h in range(heads):
            c = lanes((cols[p] * heads + h) * HEAD)
            own = slice(h * HEAD, (h + 1) * HEAD)
            prev = prev_ref[:, c].astype(F32)
            after = next_ref[:, c].astype(F32)
            feats = []
            for i, tap_ref in enumerate((tq, tk, tv)):
                x = x_ref.at[h, i]
                ahead = slice(REACH * i, REACH * (i + 1))
                x[PAD + rows : PAD + rows + REACH] = after[ahead]
                x[PAD + rows + REACH :] = fill
                taps = tap_ref[:, c].astype(F32)
                feats.append(conv(x, taps, raw_ref[p, i, :, own], prev[ahead], ext))
            edge = jnp.concatenate([after[3 * REACH : 4 * REACH], fill], 0).astype(BF16)
            feats.append(jnp.concatenate([raw_ref[p, 3, :, own], edge], 0))
            for i in range(3):
                e_ref[p, i, :, own] = feats[1 + i][rows:]
            for i in range(2):
                f_ref[p, i, :, own] = feats[1 + i][:rows]
            whole.append(feats)
        qs, ks, vs, gs = [jnp.concatenate([f[i][rows:] for f in whole], 0) for i in range(4)]
        scores = dot(gs, vs, 1, 1)
        scores_t = dot(vs, gs, 1, 1)
        similar_t = dot(ks, qs, 1, 1)
        eq = dot(jnp.where(edge_lower, scores, 0.0).astype(BF16), ks, 1, 0)
        ek = dot(jnp.where(edge_strict, scores_t, 0.0).astype(BF16), qs, 1, 0)
        ev = dot(jnp.where(edge_strict, similar_t, 0.0).astype(BF16), gs, 1, 0)
        for h in range(heads):
            r = slice(h * EDGE, (h + 1) * EDGE)
            q, k, v, gx = whole[h]
            q, k, v, g = q[:rows], k[:rows], v[:rows], gx[:rows]
            scores = dot(gx, v, 1, 1)
            part = dot(jnp.where(lower, scores, 0.0).astype(BF16), k, 1, 0)
            d_ref[p, h, 0, :rows] = part[:rows].astype(BF16)
            d_ref[p, h, 0, rows:] = (part[rows:] + eq[r]).astype(BF16)
            scores_t = jnp.where(upper, scores[:rows].T, 0.0).astype(BF16)
            d_ref[p, h, 1, :rows] = dot(scores_t, q, 1, 0).astype(BF16)
            d_ref[p, h, 1, rows:] = (-ek[r]).astype(BF16)
            similar_t = jnp.where(upper, dot(k, q, 1, 1), 0.0).astype(BF16)
            d_ref[p, h, 2, :rows] = dot(similar_t, g, 1, 0).astype(BF16)
            d_ref[p, h, 2, rows:] = (-ev[r]).astype(BF16)
        saves.append(copies.start(d_ref.at[p], d_hbm.at[p]))
        saves.append(copies.start(e_ref.at[p], e_hbm.at[p]))
        saves.append(copies.start(f_ref.at[p], f_hbm.at[p]))
    wait(saves)


def intra_call(peers, heads, cols, raws, prev, after, taps, behind):
    rows = raws[0].shape[0]
    ext = rows + EDGE
    width = heads * HEAD
    outs = [(peers, heads, 3, ext, HEAD), (peers, 3, EDGE, width), (peers, 2, rows, width)]
    return marked_call(
        functools.partial(intra_kernel, peers, heads),
        "intra",
        cols,
        [prev, after, *taps],
        raws,
        [pltpu.HBM(dims, BF16) for dims in outs],
        [pltpu.VMEM((peers, 4, rows, width), BF16)]
        + [pltpu.VMEM(dims, BF16) for dims in outs]
        + [
            pltpu.VMEM((heads, 3, PAD + ext, HEAD), F32),
            pltpu.SemaphoreType.DMA((peers * 7,)),
        ],
        12 * peers * heads * rows * HEAD * HEAD,
        behind,
    )


def sums_kernel(count, idx, *refs):
    s_refs, outs = refs[:count], refs[count:]
    heads = outs[0].shape[0]
    for h in range(heads):
        total = 0.0
        for r in s_refs:
            total = total + r[h].astype(F32)
        for bit, out in enumerate(outs):
            low = (idx[0] >> bit) & 1 == 0
            out[h] = jnp.where(low, total[0], total[1]).astype(BF16)


def members_kernel(order, planes, targets, idx, *refs):
    count = len(order)
    s_refs, z_refs = refs[:count], refs[count : count + planes - 1]
    outs = refs[count + planes - 1 :]
    bits = count.bit_length() - 1

    def share(condition):
        return jnp.where(condition, 1.0, 0.0)

    lower = [share((idx[0] ^ d) < idx[0]) for d in range(1, planes)]
    late = [[share(((idx[1] ^ d) >> b) & 1 == 1) for b in range(bits)] for d in targets]
    for h in range(z_refs[0].shape[0]):
        for top in range(0, HEAD, TILE):
            r = slice(top, top + TILE)
            for i in range(2):
                base = 0.0
                for z_ref, low in zip(z_refs, lower):
                    base = base + z_ref[h, r].astype(F32) * (1.0 - low if i else low)
                sums = [[s_refs[order.index(d)][h, i, r].astype(F32) for d in range(count)]]
                for b in range(bits - 1):
                    sums.append([x + y for x, y in zip(sums[b][::2], sums[b][1::2])])
                for out, d, shares in zip(outs, targets, late):
                    total = base
                    for b in range(bits):
                        weight = 1.0 - shares[b] if i else shares[b]
                        total = total + sums[b][(d >> b) ^ 1] * weight
                    out[h, i, r] = total.astype(BF16)


def grads_kernel(scale, peers, heads, alias, cols, *refs):
    tq, tk, tv, d_ref, e_ref, f_ref, g_ref = refs[:7]
    p_refs = refs[7 : 7 + peers]
    outs, (out_ref, x_ref, sems) = refs[-6:-3], refs[-3:]
    rows, width = out_ref.shape[2:]
    copies = Copies(sems)
    saves = []
    for p in range(peers):
        for h in range(heads):
            c = lanes((cols[p] * heads + h) * HEAD)
            own = slice(h * HEAD, (h + 1) * HEAD)
            vk, gq = p_refs[p][h, 0], p_refs[p][h, 1]
            kx, vx, gx = [
                jnp.concatenate([field, e_ref[p, i, :, own]], 0)
                for i, field in enumerate((f_ref[p, 0, :, own], f_ref[p, 1, :, own], g_ref[:, c]))
            ]
            d = x_ref.at[h]
            d[0] = d_ref[p, h, 0].astype(F32) + dot(gx, vk, 1, 0)
            d[1] = d_ref[p, h, 1].astype(F32) + dot(vx, gq, 1, 0)
            d[2] = d_ref[p, h, 2].astype(F32) + dot(kx, gq, 1, 1)
            for i, tap_ref in enumerate((tq, tk, tv)):
                taps = tap_ref[:, c].astype(F32) * scale
                total = taps[0:1] * d[i, 0:rows]
                for j in range(1, KERNEL):
                    total = total + taps[j : j + 1] * d[i, j : j + rows]
                out_ref[p, i, :, own] = total.astype(BF16)
        c = lanes(cols[p] * width, width)
        saves += [copies.start(out_ref.at[p, i], outs[i].at[:, c]) for i in range(3)]
    wait(saves)


def grads_call(peers, heads, scale, cols, g, intra, states, taps, outs):
    rows, total_width = g.shape
    ext = rows + EDGE
    near = [*taps, *intra, g, *states]
    remote = []
    aliases = []
    if outs is not None:
        aliases = [(len(near) + i, i) for i in range(3)]
        remote = outs
    results, _ = marked_call(
        functools.partial(grads_kernel, scale, peers, heads, outs is not None),
        "grads",
        cols,
        near,
        remote,
        [pltpu.HBM((rows, total_width), BF16)] * 3,
        [
            pltpu.VMEM((peers, 3, rows, heads * HEAD), BF16),
            pltpu.VMEM((heads, 3, ext, HEAD), F32),
            pltpu.SemaphoreType.DMA((peers * 3,)),
        ],
        6 * heads * peers * ext * HEAD * HEAD,
        aliases=aliases,
    )
    return results


def local(query_raw, key_raw, value_raw, grad_out, query_kernel, key_kernel, value_kernel):
    rows, total_width = query_raw.shape
    planes = lax.axis_size("z")
    members = CORES * lax.axis_size("y") * lax.axis_size("x")
    devices = planes * members
    scale = float(HEAD * rows * devices) ** (-0.5)
    heads = total_width // HEAD // members
    everyone = ("z", "core", "y", "x")
    plane = ("core", "y", "x")
    raws = (query_raw, key_raw, value_raw, grad_out)
    taps = (query_kernel, key_kernel, value_kernel)
    x, z = lax.axis_index("x"), lax.axis_index("z")
    me = (lax.axis_index("core") * lax.axis_size("y") + lax.axis_index("y")) * lax.axis_size("x") + x
    width_y = lax.axis_size("y")
    steps = {d: (d % 2 > 0) + (d // 2 % width_y > 0) for d in range(members)}
    direct, diagonal, near = [[d for d in steps if steps[d] == n] for n in (1, 2, 0)]
    direct.sort(key=lambda d: (d // (2 * width_y), d))
    near.reverse()
    order = [*direct, *diagonal, *near]

    def numbers(ds):
        return (me ^ jnp.array(ds, jnp.int32)).astype(jnp.int32)

    idx = jnp.stack([z, me]).astype(jnp.int32)

    def swap(field, axes, count, d):
        return lax.ppermute(field, axes, [(i, i ^ d) for i in range(count)]) if d else field

    tail, lead = pack(raws)
    prev = lax.ppermute(tail, everyone, [(i, i + 1) for i in range(devices - 1)])
    after = lax.ppermute(lead, everyone, [(i + 1, i) for i in range(devices - 1)])

    states, mark = {}, []

    def make_states(ds, mark, arrived):
        args = (numbers(ds), raws, prev, taps, mark, arrived)
        out, mark = states_call(len(ds), heads, *args)
        states.update({d: swap(s, plane, members, d) for s, d in zip(out, ds)})
        return [mark]

    intra = {}

    def make_intra(ds, mark):
        args = (numbers(ds), raws, prev, after, taps, mark)
        intra[ds[0]], mark = intra_call(len(ds), heads, *args)
        return [mark]

    others = [*near, *diagonal]
    mark = make_states(direct, mark, [])
    mark = make_states(diagonal, mark, [after])
    mark = make_states(near, mark, [states[direct[0]]])
    mark = make_intra(direct, mark)
    states = [states[d] for d in order]
    bits = (planes - 1).bit_length()
    levels, mark = marked_call(
        functools.partial(sums_kernel, members),
        "sums",
        idx,
        states,
        [],
        [shape((heads, HEAD, HEAD))] * bits,
        behind=mark,
    )
    across = [swap(levels[d.bit_length() - 1], "z", planes, d) for d in range(1, planes)]
    mark = make_intra(others, [mark])
    backs = {}
    for ds in (direct, [*diagonal, *near]):
        sent, mark = marked_call(
            functools.partial(members_kernel, order, planes, ds),
            "members",
            idx,
            [*states, *across],
            [],
            [shape((heads, 2, HEAD, HEAD))] * len(ds),
            behind=mark,
            arrived=[backs[d] for d in direct[:1] if backs],
        )
        mark = [mark]
        backs |= {d: swap(s, plane, members, d) for s, d in zip(sent, ds)}
    outs = None
    for ds in (direct, others):
        got = [backs[d] for d in ds]
        outs = grads_call(len(ds), heads, scale, numbers(ds), grad_out, intra[ds[0]], got, taps, outs)
    return tuple(outs)


def solution(mesh):
    chain, grp = mesh.shape["chain"], mesh.shape["grp"]
    sizes = (chain // CORES, CORES, grp // 2, 2)
    split = Mesh(mesh.devices.reshape(sizes), ("z", "core", "y", "x"))
    tokens = P(("z", "core", "y", "x"), None)
    return jax.shard_map(
        local,
        mesh=split,
        in_specs=(tokens,) * 4 + (P(),) * 3,
        out_specs=(tokens,) * 3,
        check_vma=False,
    )
```

```python
import functools
import math

import jax
import jax.numpy as jnp
from jax import lax
from jax.experimental import pallas as pl
from jax.experimental.pallas import tpu as pltpu
from jax.sharding import Mesh, PartitionSpec as P

HEAD = 128
KERNEL = 4
REACH = KERNEL - 1
CORES = 2
PAD = 8
TILE = 16
EDGE = 16
MIB = 1024 * 1024

F32 = jnp.float32
BF16 = jnp.bfloat16


def dot(a, b, ca, cb):
    return lax.dot_general(a, b, (((ca,), (cb,)), ((), ())), preferred_element_type=F32)


def shape(dims, dtype=BF16):
    return jax.ShapeDtypeStruct(dims, dtype)


def far(x):
    return pltpu.with_memory_space_constraint(x, pltpu.HBM)


def params(mib=20):
    return pltpu.CompilerParams(vmem_limit_bytes=mib * MIB)


def cost(flops, moved):
    return pl.CostEstimate(flops=int(flops), bytes_accessed=int(moved), transcendentals=0)


def pack_kernel(start, *refs):
    count = len(refs) - 3
    out_ref, x_ref, sems = refs[count:]
    copies = []
    for i, ref in enumerate(refs[:count]):
        first = ref.shape[0] - EDGE if start else 0
        copy = pltpu.make_async_copy(ref.at[pl.ds(first, EDGE)], x_ref.at[i], sems.at[i])
        copy.start()
        copies.append(copy)
    for copy in copies:
        copy.wait()
    parts = [x_ref[i].astype(F32)[start : start + REACH] for i in range(count)]
    fill = jnp.zeros((EDGE - REACH * count, parts[0].shape[1]), F32)
    out_ref[...] = jnp.concatenate(parts + [fill], 0).astype(BF16)


def pack(raws, start):
    width = raws[0].shape[1]
    count = len(raws)
    return pl.pallas_call(
        functools.partial(pack_kernel, start),
        in_specs=[pl.BlockSpec(memory_space=pltpu.HBM)] * count,
        out_specs=pl.BlockSpec(memory_space=pltpu.VMEM),
        out_shape=shape((EDGE, width)),
        scratch_shapes=[pltpu.VMEM((count, EDGE, width), BF16), pltpu.SemaphoreType.DMA((count,))],
        compiler_params=params(),
        cost_estimate=cost(0, 5 * 2 * EDGE * width),
        name="pack",
    )(*[far(x) for x in raws])


def lanes(start, width=HEAD):
    return pl.ds(pl.multiple_of(start, HEAD), width)


class Copies:
    def __init__(self, sems):
        self.sems, self.count = sems, 0

    def start(self, source, target):
        copy = pltpu.make_async_copy(source, target, self.sems.at[self.count])
        self.count += 1
        copy.start()
        return copy


def wait(copies):
    for copy in copies:
        copy.wait()


HBM = pl.BlockSpec(memory_space=pltpu.HBM)
VMEM = pl.BlockSpec(memory_space=pltpu.VMEM)
SMEM = pl.BlockSpec(memory_space=pltpu.SMEM)


def marked_call(
    kernel, name, cols, near, remote, outs, scratch=(), flops=0, behind=(), arrived=(), aliases=()
):
    args = [*near, *remote]
    hidden = len(behind) + len(arrived)
    total = len(args) + len(outs)

    def body(cols, *refs):
        refs[hidden + total][0] = 0
        kernel(cols, *refs[hidden : hidden + total], *refs[hidden + total + 1 :])

    def out_spec(x):
        return HBM if getattr(x, "memory_space", None) == pltpu.HBM else VMEM

    moved = sum(math.prod(x.shape) * jnp.dtype(x.dtype).itemsize for x in [*args, *outs])
    *results, mark = pl.pallas_call(
        body,
        in_specs=[SMEM] * (1 + len(behind))
        + [pl.BlockSpec(memory_space=pl.ANY)] * len(arrived)
        + [VMEM] * len(near)
        + [HBM] * len(remote),
        out_specs=[out_spec(x) for x in outs] + [SMEM],
        out_shape=[*outs, shape((1,), jnp.int32)],
        scratch_shapes=scratch,
        input_output_aliases={1 + hidden + i: o for i, o in aliases},
        compiler_params=params(),
        cost_estimate=cost(flops, moved),
        name=name,
    )(cols, *behind, *arrived, *near, *[far(x) for x in remote])
    return results, mark


def conv(x, taps, raw, before, rows):
    x[PAD - REACH : PAD] = before
    x[PAD : PAD + raw.shape[0]] = raw.astype(F32)
    mixed = taps[0:1] * x[PAD : PAD + rows]
    for j in range(1, KERNEL):
        mixed = mixed + taps[j : j + 1] * x[PAD - j : PAD - j + rows]
    return mixed.astype(BF16)


def states_kernel(peers, heads, cols, prev_ref, tq, tk, tv, *rest):
    raws, s_refs = rest[:4], rest[4:-3]
    raw_ref, x_ref, sems = rest[-3:]
    rows, width = raw_ref.shape[2:]
    copies = Copies(sems)
    loads = []
    for p in range(peers):
        c = lanes(cols[p] * width, width)
        loads.append([copies.start(raw.at[:, c], raw_ref.at[p, i]) for i, raw in enumerate(raws)])
    for p in range(peers):
        wait(loads[p])
        for h in range(heads):
            c = lanes((cols[p] * heads + h) * HEAD)
            own = slice(h * HEAD, (h + 1) * HEAD)
            prev = prev_ref[:, c].astype(F32)
            qf, kf, vf = [
                conv(
                    x_ref.at[(p * heads + h) % 4, i],
                    tap_ref[:, c].astype(F32),
                    raw_ref[p, i, :, own],
                    prev[REACH * i : REACH * (i + 1)],
                    rows,
                )
                for i, tap_ref in enumerate((tq, tk, tv))
            ]
            s_refs[p][h, 0] = dot(vf, kf, 0, 0).astype(BF16)
            s_refs[p][h, 1] = dot(raw_ref[p, 3, :, own], qf, 0, 0).astype(BF16)


def states_call(peers, heads, cols, raws, prev, taps, behind, arrived):
    rows = raws[0].shape[0]
    return marked_call(
        functools.partial(states_kernel, peers, heads),
        "states",
        cols,
        [prev, *taps],
        raws,
        [shape((heads, 2, HEAD, HEAD))] * peers,
        [
            pltpu.VMEM((peers, 4, rows, heads * HEAD), BF16),
            pltpu.VMEM((4, 3, PAD + rows, HEAD), F32),
            pltpu.SemaphoreType.DMA((peers * 4,)),
        ],
        4 * peers * heads * rows * HEAD * HEAD,
        behind,
        arrived,
    )


def intra_kernel(
    peers, heads, cols, prev_ref, next_ref, tq, tk, tv, q_hbm, k_hbm, v_hbm, g_hbm,
    d_hbm, e_hbm, f_hbm, raw_ref, d_ref, e_ref, f_ref, x_ref, sems,
):
    rows, width = raw_ref.shape[2:]
    ext = rows + EDGE
    copies = Copies(sems)
    loads = []
    for p in range(peers):
        c = lanes(cols[p] * width, width)
        raws = (q_hbm, k_hbm, v_hbm, g_hbm)
        loads.append([copies.start(raw.at[:, c], raw_ref.at[p, i]) for i, raw in enumerate(raws)])

    def order(dims):
        return lax.broadcasted_iota(jnp.int32, dims, 0), lax.broadcasted_iota(jnp.int32, dims, 1)

    row, col = order((heads * EDGE, heads * EDGE))
    same = row // EDGE == col // EDGE
    edge_lower = same & (row >= col)
    edge_strict = same & (col < row)
    row, col = order((ext, rows))
    lower = row >= col
    row, col = order((rows, rows))
    upper = col >= row
    fill = jnp.zeros((EDGE - REACH, HEAD), F32)
    saves = []
    for p in range(peers):
        wait(loads[p])
        whole = []
        for h in range(heads):
            c = lanes((cols[p] * heads + h) * HEAD)
            own = slice(h * HEAD, (h + 1) * HEAD)
            prev = prev_ref[:, c].astype(F32)
            after = next_ref[:, c].astype(F32)
            feats = []
            for i, tap_ref in enumerate((tq, tk, tv)):
                x = x_ref.at[h, i]
                ahead = slice(REACH * i, REACH * (i + 1))
                x[PAD + rows : PAD + rows + REACH] = after[ahead]
                x[PAD + rows + REACH :] = fill
                taps = tap_ref[:, c].astype(F32)
                feats.append(conv(x, taps, raw_ref[p, i, :, own], prev[ahead], ext))
            edge = jnp.concatenate([after[3 * REACH : 4 * REACH], fill], 0).astype(BF16)
            feats.append(jnp.concatenate([raw_ref[p, 3, :, own], edge], 0))
            for i in range(3):
                e_ref[p, i, :, own] = feats[1 + i][rows:]
            for i in range(2):
                f_ref[p, i, :, own] = feats[1 + i][:rows]
            whole.append(feats)
        qs, ks, vs, gs = [jnp.concatenate([f[i][rows:] for f in whole], 0) for i in range(4)]
        scores = dot(gs, vs, 1, 1)
        scores_t = dot(vs, gs, 1, 1)
        similar_t = dot(ks, qs, 1, 1)
        eq = dot(jnp.where(edge_lower, scores, 0.0).astype(BF16), ks, 1, 0)
        ek = dot(jnp.where(edge_strict, scores_t, 0.0).astype(BF16), qs, 1, 0)
        ev = dot(jnp.where(edge_strict, similar_t, 0.0).astype(BF16), gs, 1, 0)
        for h in range(heads):
            r = slice(h * EDGE, (h + 1) * EDGE)
            q, k, v, gx = whole[h]
            q, k, v, g = q[:rows], k[:rows], v[:rows], gx[:rows]
            scores = dot(gx, v, 1, 1)
            part = dot(jnp.where(lower, scores, 0.0).astype(BF16), k, 1, 0)
            d_ref[p, h, 0, :rows] = part[:rows].astype(BF16)
            d_ref[p, h, 0, rows:] = (part[rows:] + eq[r]).astype(BF16)
            scores_t = jnp.where(upper, scores[:rows].T, 0.0).astype(BF16)
            d_ref[p, h, 1, :rows] = dot(scores_t, q, 1, 0).astype(BF16)
            d_ref[p, h, 1, rows:] = (-ek[r]).astype(BF16)
            similar_t = jnp.where(upper, dot(k, q, 1, 1), 0.0).astype(BF16)
            d_ref[p, h, 2, :rows] = dot(similar_t, g, 1, 0).astype(BF16)
            d_ref[p, h, 2, rows:] = (-ev[r]).astype(BF16)
        saves.append(copies.start(d_ref.at[p], d_hbm.at[p]))
        saves.append(copies.start(e_ref.at[p], e_hbm.at[p]))
        saves.append(copies.start(f_ref.at[p], f_hbm.at[p]))
    wait(saves)


def intra_call(peers, heads, cols, raws, prev, after, taps, behind):
    rows = raws[0].shape[0]
    ext = rows + EDGE
    width = heads * HEAD
    outs = [(peers, heads, 3, ext, HEAD), (peers, 3, EDGE, width), (peers, 2, rows, width)]
    return marked_call(
        functools.partial(intra_kernel, peers, heads),
        "intra",
        cols,
        [prev, after, *taps],
        raws,
        [pltpu.HBM(dims, BF16) for dims in outs],
        [pltpu.VMEM((peers, 4, rows, width), BF16)]
        + [pltpu.VMEM(dims, BF16) for dims in outs]
        + [
            pltpu.VMEM((heads, 3, PAD + ext, HEAD), F32),
            pltpu.SemaphoreType.DMA((peers * 7,)),
        ],
        12 * peers * heads * rows * HEAD * HEAD,
        behind,
    )


def sums_kernel(count, idx, *refs):
    s_refs, outs = refs[:count], refs[count:]
    heads = outs[0].shape[0]
    for h in range(heads):
        total = 0.0
        for r in s_refs:
            total = total + r[h].astype(F32)
        for bit, out in enumerate(outs):
            low = (idx[0] >> bit) & 1 == 0
            out[h] = jnp.where(low, total[0], total[1]).astype(BF16)


def members_kernel(order, planes, targets, idx, *refs):
    count = len(order)
    s_refs, z_refs = refs[:count], refs[count : count + planes - 1]
    outs = refs[count + planes - 1 :]
    bits = count.bit_length() - 1

    def share(condition):
        return jnp.where(condition, 1.0, 0.0)

    lower = [share((idx[0] ^ d) < idx[0]) for d in range(1, planes)]
    late = [[share(((idx[1] ^ d) >> b) & 1 == 1) for b in range(bits)] for d in targets]
    for h in range(z_refs[0].shape[0]):
        for top in range(0, HEAD, TILE):
            r = slice(top, top + TILE)
            for i in range(2):
                base = 0.0
                for z_ref, low in zip(z_refs, lower):
                    base = base + z_ref[h, r].astype(F32) * (1.0 - low if i else low)
                sums = [[s_refs[order.index(d)][h, i, r].astype(F32) for d in range(count)]]
                for b in range(bits - 1):
                    sums.append([x + y for x, y in zip(sums[b][::2], sums[b][1::2])])
                for out, d, shares in zip(outs, targets, late):
                    total = base
                    for b in range(bits):
                        weight = 1.0 - shares[b] if i else shares[b]
                        total = total + sums[b][(d >> b) ^ 1] * weight
                    out[h, i, r] = total.astype(BF16)


def grads_kernel(scale, peers, heads, first, cols, *refs):
    tq, tk, tv, d_ref, e_ref, f_ref, g_ref = refs[:7]
    p_refs = refs[7 : 7 + peers]
    outs, (out_ref, x_ref, sems) = refs[-6:-3], refs[-3:]
    rows, width = out_ref.shape[2:]
    copies = Copies(sems)
    saves = []
    for p in range(peers):
        for h in range(heads):
            c = lanes((cols[p] * heads + h) * HEAD)
            own = slice(h * HEAD, (h + 1) * HEAD)
            vk, gq = p_refs[p][h, 0], p_refs[p][h, 1]
            kx, vx, gx = [
                jnp.concatenate([field, e_ref[first + p, i, :, own]], 0)
                for i, field in enumerate(
                    (f_ref[first + p, 0, :, own], f_ref[first + p, 1, :, own], g_ref[:, c])
                )
            ]
            d = x_ref.at[h]
            d[0] = d_ref[first + p, h, 0].astype(F32) + dot(gx, vk, 1, 0)
            d[1] = d_ref[first + p, h, 1].astype(F32) + dot(vx, gq, 1, 0)
            d[2] = d_ref[first + p, h, 2].astype(F32) + dot(kx, gq, 1, 1)
            for i, tap_ref in enumerate((tq, tk, tv)):
                taps = tap_ref[:, c].astype(F32) * scale
                total = taps[0:1] * d[i, 0:rows]
                for j in range(1, KERNEL):
                    total = total + taps[j : j + 1] * d[i, j : j + rows]
                out_ref[p, i, :, own] = total.astype(BF16)
        c = lanes(cols[p] * width, width)
        saves += [copies.start(out_ref.at[p, i], outs[i].at[:, c]) for i in range(3)]
    wait(saves)


def grads_call(peers, heads, scale, cols, g, intra, first, states, taps, outs):
    rows, total_width = g.shape
    ext = rows + EDGE
    near = [*taps, *intra, g, *states]
    remote = []
    aliases = []
    if outs is not None:
        aliases = [(len(near) + i, i) for i in range(3)]
        remote = outs
    results, _ = marked_call(
        functools.partial(grads_kernel, scale, peers, heads, first),
        "grads",
        cols,
        near,
        remote,
        [pltpu.HBM((rows, total_width), BF16)] * 3,
        [
            pltpu.VMEM((peers, 3, rows, heads * HEAD), BF16),
            pltpu.VMEM((heads, 3, ext, HEAD), F32),
            pltpu.SemaphoreType.DMA((peers * 3,)),
        ],
        6 * heads * peers * ext * HEAD * HEAD,
        aliases=aliases,
    )
    return results


def local(query_raw, key_raw, value_raw, grad_out, query_kernel, key_kernel, value_kernel):
    rows, total_width = query_raw.shape
    planes = lax.axis_size("z")
    members = CORES * lax.axis_size("y") * lax.axis_size("x")
    devices = planes * members
    scale = float(HEAD * rows * devices) ** (-0.5)
    heads = total_width // HEAD // members
    everyone = ("z", "core", "y", "x")
    plane = ("core", "y", "x")
    raws = (query_raw, key_raw, value_raw, grad_out)
    taps = (query_kernel, key_kernel, value_kernel)
    x, z = lax.axis_index("x"), lax.axis_index("z")
    me = (lax.axis_index("core") * lax.axis_size("y") + lax.axis_index("y")) * lax.axis_size("x") + x
    width_y = lax.axis_size("y")
    steps = {d: (d % 2 > 0) + (d // 2 % width_y > 0) for d in range(members)}
    direct, diagonal, near = [[d for d in steps if steps[d] == n] for n in (1, 2, 0)]
    direct.sort(key=lambda d: (d // (2 * width_y), d))
    near.reverse()
    order = [*direct, *diagonal, *near]

    def numbers(ds):
        return (me ^ jnp.array(ds, jnp.int32)).astype(jnp.int32)

    idx = jnp.stack([z, me]).astype(jnp.int32)

    def swap(field, axes, count, d):
        return lax.ppermute(field, axes, [(i, i ^ d) for i in range(count)]) if d else field

    tail, lead = pack(raws[:3], EDGE - REACH), pack(raws, 0)
    prev = lax.ppermute(tail, everyone, [(i, i + 1) for i in range(devices - 1)])
    after = lax.ppermute(lead, everyone, [(i + 1, i) for i in range(devices - 1)])

    states, mark = {}, []

    def make_states(ds, mark, arrived):
        args = (numbers(ds), raws, prev, taps, mark, arrived)
        out, mark = states_call(len(ds), heads, *args)
        states.update({d: swap(s, plane, members, d) for s, d in zip(out, ds)})
        return [mark]

    intra = {}

    def make_intra(ds, mark):
        args = (numbers(ds), raws, prev, after, taps, mark)
        intra[ds[0]], mark = intra_call(len(ds), heads, *args)
        return [mark]

    others = [*near, *diagonal]
    mark = make_states(direct, mark, [])
    mark = make_states(diagonal, mark, [after])
    mark = make_states(near, mark, [states[direct[0]]])
    mark = make_intra(direct, mark)
    states = [states[d] for d in order]
    bits = (planes - 1).bit_length()
    levels, mark = marked_call(
        functools.partial(sums_kernel, members),
        "sums",
        idx,
        states,
        [],
        [shape((heads, HEAD, HEAD))] * bits,
        behind=mark,
    )
    across = [swap(levels[d.bit_length() - 1], "z", planes, d) for d in range(1, planes)]
    mark = make_intra(others, [mark])
    backs = {}
    for ds in (direct, [*diagonal, *near]):
        sent, mark = marked_call(
            functools.partial(members_kernel, order, planes, ds),
            "members",
            idx,
            [*states, *across],
            [],
            [shape((heads, 2, HEAD, HEAD))] * len(ds),
            behind=mark,
            arrived=[backs[d] for d in direct[:1] if backs],
        )
        mark = [mark]
        backs |= {d: swap(s, plane, members, d) for s, d in zip(sent, ds)}
    outs = None
    for ds, group in ((direct, direct), (near, others), (diagonal, others)):
        got = [backs[d] for d in ds]
        args = (grad_out, intra[group[0]], group.index(ds[0]), got, taps, outs)
        outs = grads_call(len(ds), heads, scale, numbers(ds), *args)
    return tuple(outs)


def solution(mesh):
    chain, grp = mesh.shape["chain"], mesh.shape["grp"]
    sizes = (chain // CORES, CORES, grp // 2, 2)
    split = Mesh(mesh.devices.reshape(sizes), ("z", "core", "y", "x"))
    tokens = P(("z", "core", "y", "x"), None)
    return jax.shard_map(
        local,
        mesh=split,
        in_specs=(tokens,) * 4 + (P(),) * 3,
        out_specs=(tokens,) * 3,
        check_vma=False,
    )
```

```python
import functools
import math

import jax
import jax.numpy as jnp
from jax import lax
from jax.experimental import pallas as pl
from jax.experimental.pallas import tpu as pltpu
from jax.sharding import Mesh, PartitionSpec as P

HEAD = 128
KERNEL = 4
REACH = KERNEL - 1
CORES = 2
PAD = 8
TILE = 16
EDGE = 16
MIB = 1024 * 1024

F32 = jnp.float32
BF16 = jnp.bfloat16


def dot(a, b, ca, cb):
    return lax.dot_general(a, b, (((ca,), (cb,)), ((), ())), preferred_element_type=F32)


def shape(dims, dtype=BF16):
    return jax.ShapeDtypeStruct(dims, dtype)


def far(x):
    return pltpu.with_memory_space_constraint(x, pltpu.HBM)


def params(mib=20):
    return pltpu.CompilerParams(vmem_limit_bytes=mib * MIB)


def cost(flops, moved):
    return pl.CostEstimate(flops=int(flops), bytes_accessed=int(moved), transcendentals=0)


def pack_kernel(start, *refs):
    count = len(refs) - 3
    out_ref, x_ref, sems = refs[count:]
    copies = []
    for i, ref in enumerate(refs[:count]):
        first = ref.shape[0] - EDGE if start else 0
        copy = pltpu.make_async_copy(ref.at[pl.ds(first, EDGE)], x_ref.at[i], sems.at[i])
        copy.start()
        copies.append(copy)
    for copy in copies:
        copy.wait()
    parts = [x_ref[i].astype(F32)[start : start + REACH] for i in range(count)]
    fill = jnp.zeros((EDGE - REACH * count, parts[0].shape[1]), F32)
    out_ref[...] = jnp.concatenate(parts + [fill], 0).astype(BF16)


def pack(raws, start):
    width = raws[0].shape[1]
    count = len(raws)
    return pl.pallas_call(
        functools.partial(pack_kernel, start),
        in_specs=[pl.BlockSpec(memory_space=pltpu.HBM)] * count,
        out_specs=pl.BlockSpec(memory_space=pltpu.VMEM),
        out_shape=shape((EDGE, width)),
        scratch_shapes=[pltpu.VMEM((count, EDGE, width), BF16), pltpu.SemaphoreType.DMA((count,))],
        compiler_params=params(),
        cost_estimate=cost(0, 5 * 2 * EDGE * width),
        name="pack",
    )(*[far(x) for x in raws])


def lanes(start, width=HEAD):
    return pl.ds(pl.multiple_of(start, HEAD), width)


class Copies:
    def __init__(self, sems):
        self.sems, self.count = sems, 0

    def start(self, source, target):
        copy = pltpu.make_async_copy(source, target, self.sems.at[self.count])
        self.count += 1
        copy.start()
        return copy


def wait(copies):
    for copy in copies:
        copy.wait()


HBM = pl.BlockSpec(memory_space=pltpu.HBM)
VMEM = pl.BlockSpec(memory_space=pltpu.VMEM)
SMEM = pl.BlockSpec(memory_space=pltpu.SMEM)


def marked_call(
    kernel, name, cols, near, remote, outs, scratch=(), flops=0, behind=(), arrived=(), aliases=()
):
    args = [*near, *remote]
    hidden = len(behind) + len(arrived)
    total = len(args) + len(outs)

    def body(cols, *refs):
        refs[hidden + total][0] = 0
        kernel(cols, *refs[hidden : hidden + total], *refs[hidden + total + 1 :])

    def out_spec(x):
        return HBM if getattr(x, "memory_space", None) == pltpu.HBM else VMEM

    moved = sum(math.prod(x.shape) * jnp.dtype(x.dtype).itemsize for x in [*args, *outs])
    *results, mark = pl.pallas_call(
        body,
        in_specs=[SMEM] * (1 + len(behind))
        + [pl.BlockSpec(memory_space=pl.ANY)] * len(arrived)
        + [VMEM] * len(near)
        + [HBM] * len(remote),
        out_specs=[out_spec(x) for x in outs] + [SMEM],
        out_shape=[*outs, shape((1,), jnp.int32)],
        scratch_shapes=scratch,
        input_output_aliases={1 + hidden + i: o for i, o in aliases},
        compiler_params=params(),
        cost_estimate=cost(flops, moved),
        name=name,
    )(cols, *behind, *arrived, *near, *[far(x) for x in remote])
    return results, mark


def conv(x, taps, raw, before, rows):
    x[PAD - REACH : PAD] = before
    x[PAD : PAD + raw.shape[0]] = raw.astype(F32)
    mixed = taps[0:1] * x[PAD : PAD + rows]
    for j in range(1, KERNEL):
        mixed = mixed + taps[j : j + 1] * x[PAD - j : PAD - j + rows]
    return mixed.astype(BF16)


def states_kernel(peers, heads, cols, prev_ref, tq, tk, tv, *rest):
    raws, s_refs = rest[:4], rest[4:-3]
    raw_ref, x_ref, sems = rest[-3:]
    rows, width = raw_ref.shape[2:]
    copies = Copies(sems)
    loads = []
    for p in range(peers):
        c = lanes(cols[p] * width, width)
        loads.append([copies.start(raw.at[:, c], raw_ref.at[p, i]) for i, raw in enumerate(raws)])
    for p in range(peers):
        wait(loads[p])
        for h in range(heads):
            c = lanes((cols[p] * heads + h) * HEAD)
            own = slice(h * HEAD, (h + 1) * HEAD)
            prev = prev_ref[:, c].astype(F32)
            qf, kf, vf = [
                conv(
                    x_ref.at[(p * heads + h) % 4, i],
                    tap_ref[:, c].astype(F32),
                    raw_ref[p, i, :, own],
                    prev[REACH * i : REACH * (i + 1)],
                    rows,
                )
                for i, tap_ref in enumerate((tq, tk, tv))
            ]
            s_refs[p][h, 0] = dot(vf, kf, 0, 0).astype(BF16)
            s_refs[p][h, 1] = dot(raw_ref[p, 3, :, own], qf, 0, 0).astype(BF16)


def states_call(peers, heads, cols, raws, prev, taps, behind, arrived):
    rows = raws[0].shape[0]
    return marked_call(
        functools.partial(states_kernel, peers, heads),
        "states",
        cols,
        [prev, *taps],
        raws,
        [shape((heads, 2, HEAD, HEAD))] * peers,
        [
            pltpu.VMEM((peers, 4, rows, heads * HEAD), BF16),
            pltpu.VMEM((4, 3, PAD + rows, HEAD), F32),
            pltpu.SemaphoreType.DMA((peers * 4,)),
        ],
        4 * peers * heads * rows * HEAD * HEAD,
        behind,
        arrived,
    )


def intra_kernel(
    peers, heads, cols, prev_ref, next_ref, tq, tk, tv, q_hbm, k_hbm, v_hbm, g_hbm,
    d_hbm, e_hbm, f_hbm, raw_ref, d_ref, e_ref, f_ref, x_ref, sems,
):
    rows, width = raw_ref.shape[2:]
    ext = rows + EDGE
    copies = Copies(sems)
    loads = []
    for p in range(peers):
        c = lanes(cols[p] * width, width)
        raws = (q_hbm, k_hbm, v_hbm, g_hbm)
        loads.append([copies.start(raw.at[:, c], raw_ref.at[p, i]) for i, raw in enumerate(raws)])

    def order(dims):
        return lax.broadcasted_iota(jnp.int32, dims, 0), lax.broadcasted_iota(jnp.int32, dims, 1)

    row, col = order((heads * EDGE, heads * EDGE))
    same = row // EDGE == col // EDGE
    edge_lower = same & (row >= col)
    edge_strict = same & (col < row)
    row, col = order((ext, rows))
    lower = row >= col
    row, col = order((rows, rows))
    upper = col >= row
    fill = jnp.zeros((EDGE - REACH, HEAD), F32)
    saves = []
    for p in range(peers):
        wait(loads[p])
        whole = []
        for h in range(heads):
            c = lanes((cols[p] * heads + h) * HEAD)
            own = slice(h * HEAD, (h + 1) * HEAD)
            prev = prev_ref[:, c].astype(F32)
            after = next_ref[:, c].astype(F32)
            feats = []
            for i, tap_ref in enumerate((tq, tk, tv)):
                x = x_ref.at[h, i]
                ahead = slice(REACH * i, REACH * (i + 1))
                x[PAD + rows : PAD + rows + REACH] = after[ahead]
                x[PAD + rows + REACH :] = fill
                taps = tap_ref[:, c].astype(F32)
                feats.append(conv(x, taps, raw_ref[p, i, :, own], prev[ahead], ext))
            edge = jnp.concatenate([after[3 * REACH : 4 * REACH], fill], 0).astype(BF16)
            feats.append(jnp.concatenate([raw_ref[p, 3, :, own], edge], 0))
            for i in range(3):
                e_ref[p, i, :, own] = feats[1 + i][rows:]
            for i in range(2):
                f_ref[p, i, :, own] = feats[1 + i][:rows]
            whole.append(feats)
        qs, ks, vs, gs = [jnp.concatenate([f[i][rows:] for f in whole], 0) for i in range(4)]
        scores = dot(gs, vs, 1, 1)
        scores_t = dot(vs, gs, 1, 1)
        similar_t = dot(ks, qs, 1, 1)
        eq = dot(jnp.where(edge_lower, scores, 0.0).astype(BF16), ks, 1, 0)
        ek = dot(jnp.where(edge_strict, scores_t, 0.0).astype(BF16), qs, 1, 0)
        ev = dot(jnp.where(edge_strict, similar_t, 0.0).astype(BF16), gs, 1, 0)
        for h in range(heads):
            r = slice(h * EDGE, (h + 1) * EDGE)
            q, k, v, gx = whole[h]
            q, k, v, g = q[:rows], k[:rows], v[:rows], gx[:rows]
            scores = dot(gx, v, 1, 1)
            part = dot(jnp.where(lower, scores, 0.0).astype(BF16), k, 1, 0)
            d_ref[p, h, 0, :rows] = part[:rows].astype(BF16)
            d_ref[p, h, 0, rows:] = (part[rows:] + eq[r]).astype(BF16)
            scores_t = jnp.where(upper, scores[:rows].T, 0.0).astype(BF16)
            d_ref[p, h, 1, :rows] = dot(scores_t, q, 1, 0).astype(BF16)
            d_ref[p, h, 1, rows:] = (-ek[r]).astype(BF16)
            similar_t = jnp.where(upper, dot(k, q, 1, 1), 0.0).astype(BF16)
            d_ref[p, h, 2, :rows] = dot(similar_t, g, 1, 0).astype(BF16)
            d_ref[p, h, 2, rows:] = (-ev[r]).astype(BF16)
        saves.append(copies.start(d_ref.at[p], d_hbm.at[p]))
        saves.append(copies.start(e_ref.at[p], e_hbm.at[p]))
        saves.append(copies.start(f_ref.at[p], f_hbm.at[p]))
    wait(saves)


def intra_call(peers, heads, cols, raws, prev, after, taps, behind):
    rows = raws[0].shape[0]
    ext = rows + EDGE
    width = heads * HEAD
    outs = [(peers, heads, 3, ext, HEAD), (peers, 3, EDGE, width), (peers, 2, rows, width)]
    return marked_call(
        functools.partial(intra_kernel, peers, heads),
        "intra",
        cols,
        [prev, after, *taps],
        raws,
        [pltpu.HBM(dims, BF16) for dims in outs],
        [pltpu.VMEM((peers, 4, rows, width), BF16)]
        + [pltpu.VMEM(dims, BF16) for dims in outs]
        + [
            pltpu.VMEM((heads, 3, PAD + ext, HEAD), F32),
            pltpu.SemaphoreType.DMA((peers * 7,)),
        ],
        12 * peers * heads * rows * HEAD * HEAD,
        behind,
    )


def sums_kernel(count, idx, *refs):
    s_refs, outs = refs[:count], refs[count:]
    heads = outs[0].shape[0]
    for h in range(heads):
        total = 0.0
        for r in s_refs:
            total = total + r[h].astype(F32)
        for bit, out in enumerate(outs):
            low = (idx[0] >> bit) & 1 == 0
            out[h] = jnp.where(low, total[0], total[1]).astype(BF16)


def members_kernel(order, planes, targets, idx, *refs):
    count = len(order)
    s_refs, z_refs = refs[:count], refs[count : count + planes - 1]
    outs = refs[count + planes - 1 :]
    bits = count.bit_length() - 1

    def share(condition):
        return jnp.where(condition, 1.0, 0.0)

    lower = [share((idx[0] ^ d) < idx[0]) for d in range(1, planes)]
    late = [[share(((idx[1] ^ d) >> b) & 1 == 1) for b in range(bits)] for d in targets]
    for h in range(z_refs[0].shape[0]):
        for top in range(0, HEAD, TILE):
            r = slice(top, top + TILE)
            for i in range(2):
                base = 0.0
                for z_ref, low in zip(z_refs, lower):
                    base = base + z_ref[h, r].astype(F32) * (1.0 - low if i else low)
                sums = [[s_refs[order.index(d)][h, i, r].astype(F32) for d in range(count)]]
                for b in range(bits - 1):
                    sums.append([x + y for x, y in zip(sums[b][::2], sums[b][1::2])])
                for out, d, shares in zip(outs, targets, late):
                    total = base
                    for b in range(bits):
                        weight = 1.0 - shares[b] if i else shares[b]
                        total = total + sums[b][(d >> b) ^ 1] * weight
                    out[h, i, r] = total.astype(BF16)


def grads_kernel(scale, peers, heads, first, cols, *refs):
    tq, tk, tv, d_ref, e_ref, f_ref, g_ref = refs[:7]
    p_refs = refs[7 : 7 + peers]
    outs, (out_ref, x_ref, sems) = refs[-6:-3], refs[-3:]
    rows = out_ref.shape[2]
    copies = Copies(sems)
    saves = []
    for p in range(peers):
        for h in range(heads):
            c = lanes((cols[p] * heads + h) * HEAD)
            own = slice(h * HEAD, (h + 1) * HEAD)
            vk, gq = p_refs[p][h, 0], p_refs[p][h, 1]
            kx, vx, gx = [
                jnp.concatenate([field, e_ref[first + p, i, :, own]], 0)
                for i, field in enumerate(
                    (f_ref[first + p, 0, :, own], f_ref[first + p, 1, :, own], g_ref[:, c])
                )
            ]
            d = x_ref.at[h]
            d[0] = d_ref[first + p, h, 0].astype(F32) + dot(gx, vk, 1, 0)
            d[1] = d_ref[first + p, h, 1].astype(F32) + dot(vx, gq, 1, 0)
            d[2] = d_ref[first + p, h, 2].astype(F32) + dot(kx, gq, 1, 1)
            for i, tap_ref in enumerate((tq, tk, tv)):
                taps = tap_ref[:, c].astype(F32) * scale
                total = taps[0:1] * d[i, 0:rows]
                for j in range(1, KERNEL):
                    total = total + taps[j : j + 1] * d[i, j : j + rows]
                out_ref[p, i, :, own] = total.astype(BF16)
                saves.append(copies.start(out_ref.at[p, i, :, own], outs[i].at[:, c]))
    wait(saves)


def grads_call(peers, heads, scale, cols, g, intra, first, states, taps, outs):
    rows, total_width = g.shape
    ext = rows + EDGE
    near = [*taps, *intra, g, *states]
    remote = []
    aliases = []
    if outs is not None:
        aliases = [(len(near) + i, i) for i in range(3)]
        remote = outs
    results, _ = marked_call(
        functools.partial(grads_kernel, scale, peers, heads, first),
        "grads",
        cols,
        near,
        remote,
        [pltpu.HBM((rows, total_width), BF16)] * 3,
        [
            pltpu.VMEM((peers, 3, rows, heads * HEAD), BF16),
            pltpu.VMEM((heads, 3, ext, HEAD), F32),
            pltpu.SemaphoreType.DMA((peers * heads * 3,)),
        ],
        6 * heads * peers * ext * HEAD * HEAD,
        aliases=aliases,
    )
    return results


def local(query_raw, key_raw, value_raw, grad_out, query_kernel, key_kernel, value_kernel):
    rows, total_width = query_raw.shape
    planes = lax.axis_size("z")
    members = CORES * lax.axis_size("y") * lax.axis_size("x")
    devices = planes * members
    scale = float(HEAD * rows * devices) ** (-0.5)
    heads = total_width // HEAD // members
    everyone = ("z", "core", "y", "x")
    plane = ("core", "y", "x")
    raws = (query_raw, key_raw, value_raw, grad_out)
    taps = (query_kernel, key_kernel, value_kernel)
    x, z = lax.axis_index("x"), lax.axis_index("z")
    me = (lax.axis_index("core") * lax.axis_size("y") + lax.axis_index("y")) * lax.axis_size("x") + x
    width_y = lax.axis_size("y")
    steps = {d: (d % 2 > 0) + (d // 2 % width_y > 0) for d in range(members)}
    direct, diagonal, near = [[d for d in steps if steps[d] == n] for n in (1, 2, 0)]
    direct.sort(key=lambda d: (d // (2 * width_y), d))
    near.reverse()
    order = [*direct, *diagonal, *near]

    def numbers(ds):
        return (me ^ jnp.array(ds, jnp.int32)).astype(jnp.int32)

    idx = jnp.stack([z, me]).astype(jnp.int32)

    def swap(field, axes, count, d):
        return lax.ppermute(field, axes, [(i, i ^ d) for i in range(count)]) if d else field

    tail, lead = pack(raws[:3], EDGE - REACH), pack(raws, 0)
    prev = lax.ppermute(tail, everyone, [(i, i + 1) for i in range(devices - 1)])
    after = lax.ppermute(lead, everyone, [(i + 1, i) for i in range(devices - 1)])

    states, mark = {}, []

    def make_states(ds, mark, arrived):
        args = (numbers(ds), raws, prev, taps, mark, arrived)
        out, mark = states_call(len(ds), heads, *args)
        states.update({d: swap(s, plane, members, d) for s, d in zip(out, ds)})
        return [mark]

    intra = {}

    def make_intra(ds, mark):
        args = (numbers(ds), raws, prev, after, taps, mark)
        intra[ds[0]], mark = intra_call(len(ds), heads, *args)
        return [mark]

    others = [*near, *diagonal]
    mark = make_states(direct, mark, [])
    mark = make_states(diagonal, mark, [after])
    mark = make_states(near, mark, [states[direct[0]]])
    mark = make_intra(direct, mark)
    states = [states[d] for d in order]
    bits = (planes - 1).bit_length()
    levels, mark = marked_call(
        functools.partial(sums_kernel, members),
        "sums",
        idx,
        states,
        [],
        [shape((heads, HEAD, HEAD))] * bits,
        behind=mark,
    )
    across = [swap(levels[d.bit_length() - 1], "z", planes, d) for d in range(1, planes)]
    mark = make_intra(others, [mark])
    backs = {}
    for ds in (direct, [*diagonal, *near]):
        sent, mark = marked_call(
            functools.partial(members_kernel, order, planes, ds),
            "members",
            idx,
            [*states, *across],
            [],
            [shape((heads, 2, HEAD, HEAD))] * len(ds),
            behind=mark,
            arrived=[backs[d] for d in direct[:1] if backs],
        )
        mark = [mark]
        backs |= {d: swap(s, plane, members, d) for s, d in zip(sent, ds)}
    outs = None
    for ds, group in ((direct, direct), (near, others), (diagonal, others)):
        got = [backs[d] for d in ds]
        args = (grad_out, intra[group[0]], group.index(ds[0]), got, taps, outs)
        outs = grads_call(len(ds), heads, scale, numbers(ds), *args)
    return tuple(outs)


def solution(mesh):
    chain, grp = mesh.shape["chain"], mesh.shape["grp"]
    sizes = (chain // CORES, CORES, grp // 2, 2)
    split = Mesh(mesh.devices.reshape(sizes), ("z", "core", "y", "x"))
    tokens = P(("z", "core", "y", "x"), None)
    return jax.shard_map(
        local,
        mesh=split,
        in_specs=(tokens,) * 4 + (P(),) * 3,
        out_specs=(tokens,) * 3,
        check_vma=False,
    )
```
